768 devices in a mesh: outer: 48 (over z_lo, y), dev: 16 (over x, z_hi, core).
Axes of the slice: x: 4, y: 8, z: 12 (z_hi: 2, z_lo: 6; z = z_hi * 6 + z_lo), core: 2. Of those that a mesh axis runs over, the one named last changes fastest.
Arguments:
- queries: bfloat16 [192, 6144], P('outer'), may hold values from -480 to 480
- key_cache: bfloat16 [192, 1024, 1024], P('outer', 'dev'), may hold values from -6 to 6
- value_cache: bfloat16 [192, 1024, 1024], P('outer', 'dev'), may hold values from -6 to 6
- new_key: bfloat16 [192, 1024], P('outer'), may hold values from -6 to 6
- new_value: bfloat16 [192, 1024], P('outer'), may hold values from -6 to 6
- lengths: int32 [192], P('outer'), may hold values from 256 to 1024, as said below
- experts: int32 [192, 2], P('outer'), may hold values from 0 to 7, all different within a row; in each aligned block of 4 rows (0 to 3, 4 to 7, ...) at most 2 rows name the same one
- combine: float32 [192, 2], P('outer'), may hold values from 0.2 to 1
- residual: bfloat16 [192, 6144], P('outer'), may hold values from -3 to 3
- norm_gain: float32 [6144], replicated, may hold values from 0.1 to 1.9
- w_gate: bfloat16 [6144, 73728], P(None, ('outer', 'dev')), may hold values from -0.078125 to 0.078125
- w_up: bfloat16 [6144, 73728], P(None, ('outer', 'dev')), may hold values from -0.078125 to 0.078125
- w_down: bfloat16 [73728, 6144], P(('outer', 'dev')), may hold values from -0.0625 to 0.0625
Outputs:
- mixed: bfloat16 [192, 6144], P('outer', 'dev')
The draws below stay inside these ranges and needn't reach their ends.
Inputs may be any that keep to these rules, and one draw needn't show every extreme that they name: `lengths`: some token has exactly 1024 cached positions and some exactly 256. Each row names 2 different experts; in each aligned block of 4 rows no expert is named by more than 2 rows, a bound that some block reaches.
All inputs are finite; a program needn't handle non-finite values.
Results may differ from the reference program's by a relative error of at most 0.008.
Values may be sent and summed in bfloat16 or wider, within the bound.
No kernel may reach another device: no remote copies, remote signals or barrier semaphores. Data moves between devices by JAX's collectives and lax.ppermute only.
A program may use at most 32 MiB of HBM per device.

```python
import math
import jax
import jax.numpy as jnp
import numpy as np
from jax import lax

D = 6144
HEADS = 48
KVH = 8
HD = 128
EXPERTS = 8
FFW = 9216
TOPK = 2
ROW_OUT = 4
LEN = 1024
MINLEN = 256
CAP = 2
TOKENS = 192
KVD = 1024
N_OUTER = 48


def draw_queries(key, part):
    key = jax.random.fold_in(key, 11)
    drawn = jax.random.normal(key, (TOKENS, D), jnp.float32)
    values = jnp.clip(drawn, -4.0, 4.0)
    return values.astype(jnp.bfloat16)


def draw_lengths(key, part):
    key = jax.random.fold_in(key, 5)
    values = jax.random.randint(key, (TOKENS,), MINLEN, LEN + 1)
    longest_at = jax.random.randint(jax.random.fold_in(key, 1), (), 0, TOKENS)
    shortest_at = (longest_at + 1 + jax.random.randint(jax.random.fold_in(key, 2), (), 0, TOKENS - 1)) % TOKENS
    values = values.at[longest_at].set(LEN).at[shortest_at].set(MINLEN)
    return values.astype(jnp.int32)


def levels(key, dims, pieces, low, high):
    loudness, own = 1.0, jax.random.fold_in(key, 6)
    for axis_at, shards_of in pieces:
        draws = jnp.exp(jax.random.uniform(jax.random.fold_in(own, axis_at), (shards_of,), jnp.float32, low / len(pieces), high / len(pieces)))
        loudness = loudness * jnp.repeat(draws, dims[axis_at] // shards_of).reshape([-1 if axis == axis_at else 1 for axis in range(len(dims))])
    return loudness


def routed_block(stream_key, own, number, rows, amount, top, bound, slope):
    order = jax.random.permutation(stream_key, amount)
    crowded, common = shares(amount, rows * top, bound, slope, True), shares(amount, rows * top, bound, slope, False)
    places = jnp.arange(amount)

    def named(sizes, rotation):
        used = int((sizes > 0).sum())
        fixed = max(1, used // 4)
        passed = fixed + (places - fixed + rotation * (used - fixed)) % max(1, amount - fixed)
        return jnp.zeros((amount,), jnp.int32).at[order[jnp.where(places < fixed, places, passed)]].set(jnp.asarray(sizes, jnp.int32))

    sizes = jnp.where(number % 4 == 0, named(crowded, number // 4), named(common, number - number // 4 - 1))
    mixed = jax.random.permutation(jax.random.fold_in(own, 3), amount)
    donor, sink = mixed[0:amount // 2 * 2:2], mixed[1:amount // 2 * 2:2]
    margin = jnp.minimum(sizes[donor] - 1, bound - sizes[sink]) // 2
    margin = jnp.where((donor == order[0]) | (sink == order[0]) | (sizes[sink] == 0), 0, jnp.maximum(margin, 0))
    passed = jax.random.randint(jax.random.fold_in(own, 4), (amount // 2,), 0, 1 << 20) % (margin + 1)
    sizes = sizes.at[donor].add(-passed).at[sink].add(passed)
    labels = jnp.searchsorted(jnp.cumsum(sizes), jnp.arange(rows * top), side="right").astype(jnp.int32)
    table = labels.reshape(top, rows).T
    table = table[jax.random.permutation(jax.random.fold_in(own, 1), rows)]
    rotation = jax.random.randint(jax.random.fold_in(own, 2), (rows, 1), 0, top)
    return jnp.take_along_axis(table, (jnp.arange(top)[None, :] + rotation) % top, axis=1)


def shares(number_of, total, bound, skew, full):
    loads = [(1 << 20) // math.isqrt(rank ** skew) + 1 for rank in range(1, number_of + 1)]
    largest = bound if full else min(bound, max(-(-total // number_of), total * loads[0] // sum(loads)))
    least = 1 if total - largest >= number_of - 1 else 0
    counts, surplus = [largest] + [least] * (number_of - 1), total - largest - least * (number_of - 1)
    while surplus > 0:
        free = [i for i in range(1, number_of) if counts[i] < largest] or [i for i in range(1, number_of) if counts[i] < bound]
        pool, left = sum([loads[i] for i in free]), surplus
        for i in free:
            extra = min(bound - counts[i], max(1, left * loads[i] // pool), surplus)
            counts[i] = counts[i] + extra
            surplus = surplus - extra
    return np.array(counts)


def normal_values(key, extent, scale, limit, split=(), held_as=jnp.bfloat16):
    values = scale * jax.random.normal(key, extent, jnp.float32)
    if split:
        values = values * levels(key, extent, split, -0.22, 0.18)
    return jnp.clip(values, -limit, limit).astype(held_as)


def setup_inputs(seed: int = 0) -> dict:
    streams_of = jax.random.split(jax.random.key(seed), 14)
    queries = draw_queries(jax.random.fold_in(streams_of[13], 71), 0)
    key_cache = normal_values(streams_of[1], (TOKENS, LEN, KVD), 1.0, 6.0, ((0, 48), (1, 16)))
    value_cache = normal_values(streams_of[2], (TOKENS, LEN, KVD), 1.0, 6.0, ((0, 48), (1, 16)))
    new_key = normal_values(streams_of[3], (TOKENS, KVD), 1.0, 6.0, ((0, 48),))
    new_value = normal_values(streams_of[4], (TOKENS, KVD), 1.0, 6.0, ((0, 48),))
    lengths = draw_lengths(jax.random.fold_in(streams_of[13], 71), 0)
    experts_keys = jax.random.split(jax.random.fold_in(streams_of[6], 1), TOKENS // ROW_OUT)
    experts_turns = jax.random.permutation(jax.random.fold_in(streams_of[6], 3), TOKENS // ROW_OUT)
    experts = jax.vmap(lambda own, number: routed_block(jax.random.fold_in(streams_of[6], 2), own, number, ROW_OUT, EXPERTS, TOPK, CAP, 2))(experts_keys, experts_turns).reshape((TOKENS, TOPK))
    combine = jnp.clip(0.2 + 0.8 * jax.random.uniform(streams_of[7], (TOKENS, TOPK), jnp.float32) ** levels(streams_of[7], (TOKENS, TOPK), ((0, 48),), -0.2, 0.2), 0.2, 1.0)
    residual = normal_values(streams_of[8], (TOKENS, D), 0.5, 3.0, ((0, 48),))
    norm_gain = jnp.clip(1.0 + 0.18 * jax.random.normal(streams_of[9], (D,), jnp.float32), 0.1, 1.9)
    w_gate = normal_values(streams_of[10], (D, EXPERTS * FFW), D ** -0.5, 0.078125, ((1, 768),))
    w_up = normal_values(streams_of[11], (D, EXPERTS * FFW), D ** -0.5, 0.078125, ((1, 768),))
    w_down = normal_values(streams_of[12], (EXPERTS * FFW, D), FFW ** -0.5, 0.0625, ((0, 768),))
    return {"queries": queries, "key_cache": key_cache, "value_cache": value_cache, "new_key": new_key, "new_value": new_value, "lengths": lengths, "experts": experts, "combine": combine, "residual": residual, "norm_gain": norm_gain, "w_gate": w_gate, "w_up": w_up, "w_down": w_down}


def reference(queries, key_cache, value_cache, new_key, new_value, lengths, experts, combine, residual, norm_gain, w_gate, w_up, w_down):
    score_scale = 1.0 / math.sqrt(HD)
    group_size = HEADS // KVH

    def attend(packet):
        query_row, key_rows, value_rows, own_key, own_val, length = packet
        query_heads = query_row.astype(jnp.float32).reshape(KVH, group_size, HD)
        key_heads = key_rows.astype(jnp.float32).reshape(LEN, KVH, HD)
        value_heads = value_rows.astype(jnp.float32).reshape(LEN, KVH, HD)
        scores = jnp.einsum('gjd,pgd->gjp', query_heads, key_heads) * score_scale
        own_score = jnp.einsum('gjd,gd->gj', query_heads, own_key.astype(jnp.float32).reshape(KVH, HD)) * score_scale
        is_live = (jnp.arange(LEN, dtype=jnp.int32) < length)[None, None, :]
        row_top = jnp.maximum(lax.optimization_barrier(jnp.max(jnp.where(is_live, scores, -jnp.inf), axis=-1)), own_score)
        weights = jnp.where(is_live, jnp.exp(scores - row_top[..., None]), 0.0).astype(jnp.bfloat16)
        weights = lax.optimization_barrier(weights).astype(jnp.float32)
        own_weight = lax.optimization_barrier(jnp.exp(own_score - row_top).astype(jnp.bfloat16)).astype(jnp.float32)
        summed = jnp.einsum('gjp,pgd->gjd', weights, value_heads)
        summed = summed + own_weight[..., None] * own_val.astype(jnp.float32).reshape(KVH, 1, HD)
        totals = lax.optimization_barrier(jnp.sum(weights, axis=-1)) + own_weight
        return (summed / totals[..., None]).reshape(HEADS * HD)
    attended = lax.map(attend, (queries, key_cache, value_cache, new_key, new_value, lengths))
    hidden_state = residual.astype(jnp.float32) + attended
    mean_square = lax.optimization_barrier(jnp.mean(hidden_state * hidden_state, axis=1, keepdims=True))
    normed = (hidden_state * lax.rsqrt(mean_square + 1e-05) * norm_gain).astype(jnp.bfloat16)
    chosen_ids = experts.reshape(-1)
    assign_count = chosen_ids.shape[0]
    expert_hits = (chosen_ids[:, None] == jnp.arange(EXPERTS, dtype=jnp.int32)[None, :]).astype(jnp.int32)
    blocked = expert_hits.reshape(N_OUTER, ROW_OUT * TOPK, EXPERTS)
    slot_rank = lax.optimization_barrier(jnp.sum((jnp.cumsum(blocked, axis=1) - blocked) * blocked, axis=-1)).reshape(assign_count)
    block_index = jnp.arange(assign_count, dtype=jnp.int32) // (ROW_OUT * TOPK)
    column = (block_index * CAP + slot_rank).astype(jnp.int32)
    source_row = jnp.arange(assign_count, dtype=jnp.int32) // TOPK
    table = jnp.zeros((EXPERTS, N_OUTER * CAP), jnp.int32).at[chosen_ids, column].set(source_row)

    def run_expert(expert):
        expert_rows = jnp.take(normed, table[expert], axis=0)
        gate_block = lax.dynamic_slice_in_dim(w_gate, expert * FFW, FFW, 1)
        up_block = lax.dynamic_slice_in_dim(w_up, expert * FFW, FFW, 1)
        down_block = lax.dynamic_slice_in_dim(w_down, expert * FFW, FFW, 0)
        gate_sum = jnp.dot(expert_rows, gate_block, preferred_element_type=jnp.float32)
        up_sum = jnp.dot(expert_rows, up_block, preferred_element_type=jnp.float32)
        activation = (jax.nn.silu(gate_sum) * up_sum).astype(jnp.bfloat16)
        return jnp.dot(activation, down_block, preferred_element_type=jnp.float32)
    outputs = lax.map(run_expert, jnp.arange(EXPERTS, dtype=jnp.int32))
    picked = outputs[chosen_ids, column].reshape(TOKENS, TOPK, D)
    mixed = hidden_state + lax.optimization_barrier(jnp.sum(combine[..., None] * picked, axis=1))
    return mixed.astype(jnp.bfloat16)
```

```python
import math

import jax
import jax.numpy as jnp
from jax import lax
from jax.sharding import Mesh
from jax.sharding import PartitionSpec as P

HEADS = 48
KVH = 8
HD = 128
EXPERTS = 8
TOPK = 2
CAP = 2
DEAD = -1e30

OUTER = ("zl", "y")
DEV = ("x", "zh", "c")


def two_parts(v):
    high = lax.reduce_precision(v, 8, 7)
    low = lax.reduce_precision(v - high, 8, 7)
    return high, low


def body(
    queries,
    key_cache,
    value_cache,
    new_key,
    new_value,
    lengths,
    experts,
    combine,
    residual,
    norm_gain,
    w_gate,
    w_up,
    w_down,
):
    bf16, f32 = jnp.bfloat16, jnp.float32
    rows, width = residual.shape
    group = HEADS // KVH
    nx, nz, nc = (lax.axis_size(a) for a in DEV)
    dev_count = nx * nz * nc
    outer_count = lax.axis_size("zl") * lax.axis_size("y")
    copies = outer_count // EXPERTS
    at_x, at_z, at_c = (lax.axis_index(a) for a in DEV)
    dev_index = (at_x * nz + at_z) * nc + at_c
    share = width // dev_count
    own_heads = HEADS // dev_count
    span = key_cache.shape[1]
    scale = 1.0 / math.sqrt(HD)

    q = queries.reshape(rows, KVH, group, HD)
    k = key_cache.reshape(rows, span, KVH, HD)
    v = value_cache.reshape(rows, span, KVH, HD)
    scores = jnp.einsum("rgjd,rpgd->rgjp", q, k, preferred_element_type=f32) * scale
    own_score = (
        jnp.einsum("rgjd,rgd->rgj", q, new_key.reshape(rows, KVH, HD), preferred_element_type=f32)
        * scale
    )
    own_score = jnp.where(dev_index == 0, own_score, DEAD)
    positions = dev_index * span + jnp.arange(span, dtype=jnp.int32)
    live = (positions[None, :] < lengths[:, None])[:, None, None, :]
    top = jnp.maximum(jnp.max(jnp.where(live, scores, DEAD), axis=-1), own_score)
    top_high, top_low = two_parts(top)
    base = top_high + top_low
    weights = jnp.where(live, jnp.exp(scores - base[..., None]), 0.0).astype(bf16)
    own_weight = jnp.where(dev_index == 0, jnp.exp(own_score - base), 0.0)
    own_weight = lax.reduce_precision(own_weight, 8, 7)
    acc = jnp.einsum("rgjp,rpgd->rgjd", weights, v, preferred_element_type=f32)
    acc = acc + own_weight[..., None] * new_value.reshape(rows, KVH, 1, HD).astype(f32)
    total = jnp.sum(weights.astype(f32), axis=-1) + own_weight
    total_high, total_low = two_parts(total)

    def by_target(a):
        a = a.reshape(rows, nx, nz, nc, own_heads, -1)
        return jnp.transpose(a, (1, 3, 0, 2, 4, 5))

    slab_rows = rows * nz * own_heads
    values = by_target(acc.reshape(rows, HEADS, HD)).reshape(nx, nc, slab_rows, HD)
    stats = jnp.stack([top_high, top_low, total_high, total_low]).reshape(4, rows, HEADS)
    stats = jnp.stack([by_target(stats[i]).reshape(nx, nc, slab_rows) for i in range(4)], axis=2)
    stats = jnp.pad(stats, ((0, 0), (0, 0), (0, 4), (0, HD - slab_rows)))
    packet = jnp.concatenate([values, stats], axis=2).astype(bf16)
    packet = jnp.broadcast_to(packet[:, None], (nx, nz, nc) + packet.shape[2:])
    packet = packet.reshape((dev_count,) + packet.shape[3:])
    arrived = lax.all_to_all(packet, DEV, split_axis=0, concat_axis=0, tiled=True)
    part = arrived[:, :slab_rows, :].astype(f32)
    info = arrived[:, slab_rows : slab_rows + 4, :slab_rows].astype(f32)
    base_of = info[:, 0] + info[:, 1]
    factor = jnp.exp(base_of - jnp.max(base_of, axis=0, keepdims=True))
    whole = jnp.sum(factor * (info[:, 2] + info[:, 3]), axis=0)
    attended = jnp.sum((factor / whole)[..., None] * part, axis=0)
    attended = attended.reshape(rows, nz, share)
    res = residual.reshape(rows, nx, nz, nc, share)
    res = lax.dynamic_slice(res, (0, at_x, 0, at_c, 0), (rows, 1, nz, 1, share))
    state = res.reshape(rows, nz, share).astype(f32) + attended
    own_state = lax.dynamic_index_in_dim(state, at_z, 1, keepdims=False)

    chosen = experts.reshape(rows * TOPK)
    hits = (chosen[:, None] == jnp.arange(EXPERTS, dtype=jnp.int32)[None, :]).astype(jnp.int32)
    rank = jnp.sum((jnp.cumsum(hits, axis=0) - hits) * hits, axis=1)
    slot = (rank[:, None] == jnp.arange(CAP, dtype=jnp.int32)[None, :]).astype(jnp.int32)
    placement = (hits[:, :, None] * slot[:, None, :]).reshape(rows, TOPK, EXPERTS, CAP)
    row_slots = jnp.sum(placement, axis=1)
    packed = jnp.einsum(
        "rec,rd->ecd",
        row_slots.astype(bf16),
        state.reshape(rows, nz * share).astype(bf16),
        preferred_element_type=f32,
    ).astype(bf16)
    outgoing = jnp.repeat(packed, copies, axis=0)
    incoming = lax.all_to_all(outgoing, OUTER, split_axis=0, concat_axis=0, tiled=True)
    slab = incoming.reshape(outer_count * CAP, nz * share)
    over_x = lax.all_gather(slab, "x", axis=0, tiled=False)
    half = nx // 2
    low_x = lax.all_gather(over_x[:half], "c", axis=0, tiled=False)
    high_x = lax.all_gather(over_x[half:], "c", axis=0, tiled=False)
    both = jnp.concatenate([low_x, high_x], axis=1)
    both = both.reshape(nc, nx, outer_count * CAP, nz, share)
    expert_state = jnp.transpose(both, (2, 1, 3, 0, 4)).reshape(outer_count * CAP, width)
    expert_state = expert_state.astype(f32)
    mean_square = jnp.mean(expert_state * expert_state, axis=1, keepdims=True)
    normed = (expert_state * lax.rsqrt(mean_square + 1e-05) * norm_gain).astype(bf16)
    gate_sum = jnp.dot(normed, w_gate, preferred_element_type=f32)
    up_sum = jnp.dot(normed, w_up, preferred_element_type=f32)
    activation = (jax.nn.silu(gate_sum) * up_sum).astype(bf16)
    partial_sum = jnp.dot(activation, w_down, preferred_element_type=f32).astype(bf16)

    cut = partial_sum.reshape(outer_count * CAP, nx, nz, nc, share)
    cut = jnp.transpose(cut, (3, 1, 0, 2, 4)).reshape(nc, nx, outer_count * CAP, nz * share)
    over_c = lax.all_to_all(cut, "c", split_axis=0, concat_axis=0, tiled=True)
    over_c = jnp.sum(over_c.astype(f32), axis=0).astype(bf16)
    from_x = lax.all_to_all(over_c, "x", split_axis=0, concat_axis=0, tiled=True)
    from_x = jnp.sum(from_x.astype(f32), axis=0)
    home = from_x.reshape(outer_count, CAP, nz, share)
    home = jnp.transpose(home, (0, 2, 1, 3)).reshape(outer_count * nz, CAP, share).astype(bf16)
    returned = lax.all_to_all(home, OUTER + ("zh",), split_axis=0, concat_axis=0, tiled=True)
    returned = returned.reshape(EXPERTS, copies * nz, CAP, share).astype(f32)
    expert_output = jnp.sum(returned, axis=1)
    mix_weights = jnp.sum(placement.astype(f32) * combine[:, :, None, None], axis=1)
    moe = jnp.einsum("rec,ecd->rd", mix_weights, expert_output, precision=lax.Precision.HIGHEST)
    return (own_state + moe).astype(bf16)


def solution(mesh):
    fine = Mesh(mesh.devices.reshape(6, 8, 4, 2, 2), OUTER + DEV)
    return jax.shard_map(
        body,
        mesh=fine,
        in_specs=(
            P(OUTER, None),
            P(OUTER, DEV, None),
            P(OUTER, DEV, None),
            P(OUTER, None),
            P(OUTER, None),
            P(OUTER),
            P(OUTER, None),
            P(OUTER, None),
            P(OUTER, None),
            P(),
            P(None, OUTER + DEV),
            P(None, OUTER + DEV),
            P(OUTER + DEV, None),
        ),
        out_specs=P(OUTER, DEV),
        check_vma=False,
    )
```

```python
import math

import jax
import jax.numpy as jnp
from jax import lax
from jax.experimental import pallas as pl
from jax.experimental.pallas import tpu as pltpu
from jax.sharding import Mesh
from jax.sharding import PartitionSpec as P

HEADS = 48
KVH = 8
HD = 128
EXPERTS = 8
TOPK = 2
CAP = 2
DEAD = -1e30

OUTER = ("zl", "y")
DEV = ("x", "zh", "c")
NX, NZ, NC = 4, 2, 2
VMEM = pl.BlockSpec(memory_space=pltpu.VMEM)
NT = (((1,), (1,)), ((), ()))


def attend_kernel(
    length_ref, q_ref, k_ref, v_ref, nk_ref, nv_ref, out_ref, q_rows, nk_rows, nv_rows, packed
):
    f32, bf16 = jnp.float32, jnp.bfloat16
    tokens = q_ref.shape[0]
    span = k_ref.shape[0] // tokens
    group = HEADS // KVH
    lines = group * tokens
    half = lines // NC
    scale = 1.0 / math.sqrt(HD)
    dev_index = (lax.axis_index("x") * NZ + lax.axis_index("zh")) * NC + lax.axis_index("c")
    queries = q_ref[...].astype(f32)
    new_keys = nk_ref[...].astype(f32)
    new_values = nv_ref[...].astype(f32)
    for head in range(HEADS):
        g = head // group
        at = slice(head * tokens, (head + 1) * tokens)
        q_rows[at, :] = queries[:, head * HD : (head + 1) * HD]
        nk_rows[at, :] = new_keys[:, g * HD : (g + 1) * HD]
        nv_rows[at, :] = new_values[:, g * HD : (g + 1) * HD]
    row = lax.broadcasted_iota(jnp.int32, (lines, tokens * span), 0) % tokens
    column = lax.broadcasted_iota(jnp.int32, (lines, tokens * span), 1)
    limit = jnp.zeros((lines, tokens * span), jnp.int32)
    for t in range(tokens):
        limit = jnp.where(row == t, length_ref[t], limit)
    live = (column // span == row) & (dev_index * span + column % span < limit)
    lane = lax.broadcasted_iota(jnp.int32, (lines, HD), 1)
    first = dev_index == 0
    for g in range(KVH):
        at = slice(g * lines, (g + 1) * lines)
        lanes = slice(g * HD, (g + 1) * HD)
        q = q_rows[at, :]
        scores = lax.dot_general(q.astype(bf16), k_ref[:, lanes], NT, preferred_element_type=f32)
        scores = jnp.where(live, scores * scale, DEAD)
        own = jnp.sum(q * nk_rows[at, :], axis=1, keepdims=True) * scale
        own = jnp.where(first, own, DEAD)
        top = jnp.maximum(jnp.max(scores, axis=1, keepdims=True), own)
        top_high = top.astype(bf16).astype(f32)
        top_low = (top - top_high).astype(bf16).astype(f32)
        base = top_high + top_low
        weights = jnp.where(live, jnp.exp(scores - base), 0.0).astype(bf16)
        own_weight = jnp.where(first, jnp.exp(own - base), 0.0).astype(bf16).astype(f32)
        acc = jnp.dot(weights, v_ref[:, lanes], preferred_element_type=f32)
        acc = acc + own_weight * nv_rows[at, :]
        total = jnp.sum(weights.astype(f32), axis=1, keepdims=True) + own_weight
        total_high = total.astype(bf16).astype(f32)
        total_low = total - total_high
        stats = jnp.where(
            lane == 0,
            top_high,
            jnp.where(lane == 1, top_low, jnp.where(lane == 2, total_high, total_low)),
        )
        x, z = g // NZ, g % NZ
        for c in range(NC):
            to = slice(z * half, (z + 1) * half)
            packed[x * NC + c, to, :HD] = acc[c * half : (c + 1) * half]
            packed[x * NC + c, to, HD:] = stats[c * half : (c + 1) * half]
    for x in range(NX):
        for c in range(NC):
            block = packed[x * NC + c].astype(bf16)
            for z in range(NZ):
                out_ref[(x * NZ + z) * NC + c] = block


def expert_kernel(low_ref, high_ref, gain_ref, gate_ref, up_ref, down_ref, out_ref):
    f32, bf16 = jnp.float32, jnp.bfloat16
    rows = low_ref.shape[2]
    share = low_ref.shape[3] // NZ
    width = gate_ref.shape[1]
    squares = jnp.zeros((rows, HD), f32)
    gate = jnp.zeros((rows, gate_ref.shape[0]), f32)
    up = jnp.zeros((rows, up_ref.shape[0]), f32)
    for x in range(NX):
        source = low_ref if x < NX // 2 else high_ref
        for c in range(NC):
            block = source[c, x % (NX // 2)]
            starts = [((x * NZ + z) * NC + c) * share for z in range(NZ)]

            def columns(ref):
                return jnp.concatenate([ref[:, s : s + share] for s in starts], axis=1)

            gate += lax.dot_general(block, columns(gate_ref), NT, preferred_element_type=f32)
            up += lax.dot_general(block, columns(up_ref), NT, preferred_element_type=f32)
            state = block.astype(f32) / columns(gain_ref)
            state = state * state
            for at in range(0, NZ * share, HD):
                squares += state[:, at : at + HD]
    factor = lax.rsqrt(jnp.sum(squares, axis=1, keepdims=True) / width + 1e-05)
    gate = gate * factor
    active = (gate / (1.0 + jnp.exp(-gate)) * (up * factor)).astype(bf16)
    for x in range(NX):
        for c in range(NC):
            for z in range(NZ):
                start = ((x * NZ + z) * NC + c) * share
                out_ref[c, x, :, z * share : (z + 1) * share] = jnp.dot(
                    active, down_ref[:, start : start + share], preferred_element_type=f32
                ).astype(bf16)


def local_attention(lengths, queries, key_cache, value_cache, new_key, new_value):
    rows, span, features = key_cache.shape
    slab_rows = HEADS // (NX * NC) * rows
    return pl.pallas_call(
        attend_kernel,
        out_shape=jax.ShapeDtypeStruct((NX * NZ * NC, slab_rows, 2 * HD), jnp.bfloat16),
        in_specs=[pl.BlockSpec(memory_space=pltpu.SMEM)] + [pl.BlockSpec()] * 5,
        out_specs=VMEM,
        scratch_shapes=[pltpu.VMEM((HEADS * rows, HD), jnp.float32)] * 3
        + [pltpu.VMEM((NX * NC, slab_rows, 2 * HD), jnp.float32)],
        compiler_params=pltpu.CompilerParams(vmem_limit_bytes=60 * 2**20),
        name="attend",
    )(
        lengths,
        queries,
        key_cache.reshape(rows * span, features),
        value_cache.reshape(rows * span, features),
        new_key,
        new_value,
    )


def merge(arrived):
    f32 = jnp.float32
    part = arrived[:, :, :HD].astype(f32)
    info = arrived[:, :, HD : HD + 4].astype(f32)
    base_of = info[:, :, 0] + info[:, :, 1]
    factor = jnp.exp(base_of - jnp.max(base_of, axis=0, keepdims=True))
    whole = jnp.sum(factor * (info[:, :, 2] + info[:, :, 3]), axis=0)
    return jnp.sum((factor / whole)[..., None] * part, axis=0)


def expert_layer(low, high, gain, gate, up, down):
    slots, features = low.shape[2:]
    return pl.pallas_call(
        expert_kernel,
        out_shape=jax.ShapeDtypeStruct((NC, NX, slots, features), jnp.bfloat16),
        in_specs=[VMEM] * 6,
        out_specs=VMEM,
        compiler_params=pltpu.CompilerParams(vmem_limit_bytes=16 * 2**20),
        name="expert",
    )(low, high, gain, gate, up, down)


def body(
    queries,
    key_cache,
    value_cache,
    new_key,
    new_value,
    lengths,
    experts,
    combine,
    residual,
    norm_gain,
    w_gate,
    w_up,
    w_down,
):
    bf16, f32 = jnp.bfloat16, jnp.float32
    rows, width = residual.shape
    dev_count = NX * NZ * NC
    outer_count = lax.axis_size("zl") * lax.axis_size("y")
    copies = outer_count // EXPERTS
    at_x, at_z, at_c = (lax.axis_index(a) for a in DEV)
    share = width // dev_count
    own_heads = HEADS // dev_count
    slots = outer_count * CAP

    packet = local_attention(lengths, queries, key_cache, value_cache, new_key, new_value)
    arrived = lax.all_to_all(packet, DEV, split_axis=0, concat_axis=0, tiled=True)
    attended = merge(arrived)
    attended = jnp.transpose(attended.reshape(NZ, own_heads, rows, HD), (2, 0, 1, 3))
    attended = attended.reshape(rows, NZ, share)
    res = residual.reshape(rows, NX, NZ, NC, share)
    res = lax.dynamic_slice(res, (0, at_x, 0, at_c, 0), (rows, 1, NZ, 1, share))
    state = res.reshape(rows, NZ, share).astype(f32) + attended
    own_state = lax.dynamic_index_in_dim(state, at_z, 1, keepdims=False)
    gain = norm_gain.reshape(NX, NZ, NC, share)
    gain = lax.dynamic_slice(gain, (at_x, 0, at_c, 0), (1, NZ, 1, share)).reshape(1, NZ, share)
    scaled = (state * gain).reshape(rows, NZ * share).astype(bf16)

    chosen = experts.reshape(rows * TOPK)
    hits = (chosen[:, None] == jnp.arange(EXPERTS, dtype=jnp.int32)[None, :]).astype(jnp.int32)
    rank = jnp.sum((jnp.cumsum(hits, axis=0) - hits) * hits, axis=1)
    slot = (rank[:, None] == jnp.arange(CAP, dtype=jnp.int32)[None, :]).astype(jnp.int32)
    placement = (hits[:, :, None] * slot[:, None, :]).reshape(rows, TOPK, EXPERTS, CAP)
    row_slots = jnp.sum(placement, axis=1)
    packed = jnp.einsum(
        "rec,rd->ecd", row_slots.astype(bf16), scaled, preferred_element_type=f32
    ).astype(bf16)
    outgoing = jnp.repeat(packed, copies, axis=0)
    incoming = lax.all_to_all(outgoing, OUTER, split_axis=0, concat_axis=0, tiled=True)
    slab = incoming.reshape(slots, NZ * share)
    over_x = lax.all_gather(slab, "x", axis=0, tiled=False)
    low = lax.all_gather(over_x[: NX // 2], "c", axis=0, tiled=False)
    high = lax.all_gather(over_x[NX // 2 :], "c", axis=0, tiled=False)
    cut = expert_layer(low, high, norm_gain.reshape(1, width), w_gate.T, w_up.T, w_down)

    over_c = lax.all_to_all(cut, "c", split_axis=0, concat_axis=0, tiled=True)
    over_c = jnp.sum(over_c.astype(f32), axis=0).astype(bf16)
    from_x = lax.all_to_all(over_c, "x", split_axis=0, concat_axis=0, tiled=True)
    from_x = jnp.sum(from_x.astype(f32), axis=0)
    home = from_x.reshape(outer_count, CAP, NZ, share)
    home = jnp.transpose(home, (0, 2, 1, 3)).reshape(outer_count * NZ, CAP, share).astype(bf16)
    returned = lax.all_to_all(home, OUTER + ("zh",), split_axis=0, concat_axis=0, tiled=True)
    returned = returned.reshape(EXPERTS, copies * NZ, CAP, share).astype(f32)
    expert_output = jnp.sum(returned, axis=1)
    mix_weights = jnp.sum(placement.astype(f32) * combine[:, :, None, None], axis=1)
    moe = jnp.einsum("rec,ecd->rd", mix_weights, expert_output, precision=lax.Precision.HIGHEST)
    return (own_state + moe).astype(bf16)


def solution(mesh):
    fine = Mesh(mesh.devices.reshape(6, 8, NX, NZ, NC), OUTER + DEV)
    return jax.shard_map(
        body,
        mesh=fine,
        in_specs=(
            P(OUTER, None),
            P(OUTER, DEV, None),
            P(OUTER, DEV, None),
            P(OUTER, None),
            P(OUTER, None),
            P(OUTER),
            P(OUTER, None),
            P(OUTER, None),
            P(OUTER, None),
            P(),
            P(None, OUTER + DEV),
            P(None, OUTER + DEV),
            P(OUTER + DEV, None),
        ),
        out_specs=P(OUTER, DEV),
        check_vma=False,
    )
```

```python
import math

import jax
import jax.numpy as jnp
from jax import lax
from jax.experimental import pallas as pl
from jax.experimental.pallas import tpu as pltpu
from jax.sharding import Mesh
from jax.sharding import PartitionSpec as P

HEADS = 48
KVH = 8
HD = 128
EXPERTS = 8
TOPK = 2
CAP = 2
DEAD = -1e30

OUTER = ("zl", "y")
DEV = ("x", "zh", "c")
NX, NZ, NC = 4, 2, 2
ANY = pl.BlockSpec(memory_space=pl.ANY)
VMEM = pl.BlockSpec(memory_space=pltpu.VMEM)
NT = (((1,), (1,)), ((), ()))


def starts_of(core, share):
    return [pl.multiple_of((i * NC + core) * share, share) for i in range(NX * NZ)]


def pack_copies(refs, out_ref, sems):
    share = refs[0].shape[1] // (NX * NZ * NC)
    return [
        pltpu.make_async_copy(
            ref.at[:, pl.ds(start, share)],
            out_ref.at[kind, :, pl.ds(i * share, share)],
            sems.at[kind, i],
        )
        for kind, ref in enumerate(refs)
        for i, start in enumerate(starts_of(1 - lax.axis_index("c"), share))
    ]


def attend_kernel(
    length_ref,
    q_ref,
    k_ref,
    v_ref,
    nk_ref,
    nv_ref,
    gate_ref,
    up_ref,
    down_ref,
    out_ref,
    other_ref,
    q_rows,
    nk_rows,
    nv_rows,
    packed,
    sems,
):
    copies = pack_copies((gate_ref, up_ref, down_ref), other_ref, sems)
    for copy in copies:
        copy.start()
    f32, bf16 = jnp.float32, jnp.bfloat16
    tokens = q_ref.shape[0]
    span = k_ref.shape[0] // tokens
    group = HEADS // KVH
    lines = group * tokens
    half = lines // NC
    scale = 1.0 / math.sqrt(HD)
    dev_index = (lax.axis_index("x") * NZ + lax.axis_index("zh")) * NC + lax.axis_index("c")
    queries = q_ref[...].astype(f32)
    new_keys = nk_ref[...].astype(f32)
    new_values = nv_ref[...].astype(f32)
    for head in range(HEADS):
        g = head // group
        at = slice(head * tokens, (head + 1) * tokens)
        q_rows[at, :] = queries[:, head * HD : (head + 1) * HD]
        nk_rows[at, :] = new_keys[:, g * HD : (g + 1) * HD]
        nv_rows[at, :] = new_values[:, g * HD : (g + 1) * HD]
    all_lines = HEADS * tokens
    row = lax.broadcasted_iota(jnp.int32, (lines, tokens * span), 0) % tokens
    column = lax.broadcasted_iota(jnp.int32, (lines, tokens * span), 1)
    limit = jnp.zeros((lines, tokens * span), jnp.int32)
    for t in range(tokens):
        limit = jnp.where(row == t, length_ref[t], limit)
    live = (column // span == row) & (dev_index * span + column % span < limit)
    live = jnp.concatenate([live.astype(f32)] * KVH, axis=0) > 0.5
    lane = lax.broadcasted_iota(jnp.int32, (all_lines, HD), 1)
    first = dev_index == 0
    q = q_rows[...]
    scores = jnp.concatenate(
        [
            lax.dot_general(
                q[g * lines : (g + 1) * lines].astype(bf16),
                k_ref[:, g * HD : (g + 1) * HD],
                NT,
                preferred_element_type=f32,
            )
            for g in range(KVH)
        ],
        axis=0,
    )
    scores = jnp.where(live, scores * scale, DEAD)
    own = jnp.sum(q * nk_rows[...], axis=1, keepdims=True) * scale
    own = jnp.where(first, own, DEAD)
    top = jnp.maximum(jnp.max(scores, axis=1, keepdims=True), own)
    top_high = top.astype(bf16).astype(f32)
    top_low = (top - top_high).astype(bf16).astype(f32)
    base = top_high + top_low
    weights = jnp.where(live, jnp.exp(scores - base), 0.0).astype(bf16)
    own_weight = jnp.where(first, jnp.exp(own - base), 0.0).astype(bf16).astype(f32)
    acc = jnp.concatenate(
        [
            jnp.dot(
                weights[g * lines : (g + 1) * lines],
                v_ref[:, g * HD : (g + 1) * HD],
                preferred_element_type=f32,
            )
            for g in range(KVH)
        ],
        axis=0,
    )
    acc = acc + own_weight * nv_rows[...]
    total = jnp.sum(weights.astype(f32), axis=1, keepdims=True) + own_weight
    total_high = total.astype(bf16).astype(f32)
    total_low = total - total_high
    stats = jnp.where(
        lane == 0,
        top_high,
        jnp.where(lane == 1, top_low, jnp.where(lane == 2, total_high, total_low)),
    )
    for x in range(NX):
        for z in range(NZ):
            for c in range(NC):
                to = slice(z * half, (z + 1) * half)
                at = ((x * NZ + z) * NC + c) * half
                packed[x * NC + c, to, :HD] = acc[at : at + half]
                packed[x * NC + c, to, HD:] = stats[at : at + half]
    for x in range(NX):
        for c in range(NC):
            block = packed[x * NC + c].astype(bf16)
            for z in range(NZ):
                out_ref[(x * NZ + z) * NC + c] = block
    for copy in copies:
        copy.wait()


def enter_kernel(state_ref, gain_ref, gate_ref, up_ref, pair_ref, out_ref, other, sem):
    f32 = jnp.float32
    rows, span = state_ref.shape[1:]
    share = span // NZ
    hidden = gate_ref.shape[0]
    at_c = lax.axis_index("c")
    fetch = pltpu.make_async_copy(pair_ref.at[1 - at_c, pl.ds(0, 2)], other, sem)
    fetch.start()
    starts = starts_of(at_c, share)

    def columns(ref, x):
        return jnp.concatenate(
            [ref[:, pl.ds(s, share)] for s in starts[x * NZ : (x + 1) * NZ]], axis=1
        )

    squares = jnp.zeros((rows, HD), f32)
    own = [jnp.zeros((rows, hidden), f32)] * 2
    for x in range(NX):
        block = state_ref[x]
        for kind, ref in enumerate((gate_ref, up_ref)):
            own[kind] += lax.dot_general(block, columns(ref, x), NT, preferred_element_type=f32)
        state = block.astype(f32) / columns(gain_ref, x)
        state = state * state
        for at in range(0, span, HD):
            squares += state[:, at : at + HD]
    total = jnp.sum(squares, axis=1, keepdims=True)
    total = jnp.broadcast_to(total, (rows, HD - hidden))
    fetch.wait()
    for kind in range(2):
        far = jnp.zeros((rows, hidden), f32)
        for x in range(NX):
            far += lax.dot_general(
                state_ref[x],
                other[kind, :, x * span : (x + 1) * span],
                NT,
                preferred_element_type=f32,
            )
        out_ref[kind * NC] = jnp.concatenate([own[kind], total], axis=1)
        out_ref[kind * NC + 1] = jnp.concatenate([far, total], axis=1)


def leave_kernel(sums_ref, down_ref, pair_ref, out_ref, other, sem):
    f32, bf16 = jnp.float32, jnp.bfloat16
    hidden, width = down_ref.shape
    share = out_ref.shape[3]
    at_c = lax.axis_index("c")
    fetch = pltpu.make_async_copy(pair_ref.at[1 - at_c, 2], other, sem)
    fetch.start()
    factor = None
    active = []
    for far in range(NC):
        gate = sums_ref[at_c, far] + sums_ref[1 - at_c, 1 - far]
        up = sums_ref[at_c, NC + far] + sums_ref[1 - at_c, NC + 1 - far]
        if factor is None:
            factor = lax.rsqrt(gate[:, HD - 1 :] / width + 1e-05)
        gate = gate[:, :hidden] * factor
        up = up[:, :hidden] * factor
        active.append((gate / (1.0 + jnp.exp(-gate)) * up).astype(bf16))
    fetch.wait()
    for i, start in enumerate(starts_of(at_c, share)):
        near = jnp.dot(active[0], down_ref[:, pl.ds(start, share)], preferred_element_type=f32)
        far = jnp.dot(active[1], other[:, i * share : (i + 1) * share], preferred_element_type=f32)
        out_ref[i // NZ, i % NZ] = (near + far).astype(bf16)


def local_attention(lengths, queries, key_cache, value_cache, new_key, new_value, gate, up, down):
    rows, span, features = key_cache.shape
    slab_rows = HEADS // (NX * NC) * rows
    hidden, width = down.shape
    return pl.pallas_call(
        attend_kernel,
        out_shape=(
            jax.ShapeDtypeStruct((NX * NZ * NC, slab_rows, 2 * HD), jnp.bfloat16),
            jax.ShapeDtypeStruct((3, hidden, width // NC), jnp.bfloat16),
        ),
        in_specs=[pl.BlockSpec(memory_space=pltpu.SMEM)] + [pl.BlockSpec()] * 5 + [ANY] * 3,
        out_specs=(VMEM, ANY),
        scratch_shapes=[pltpu.VMEM((HEADS * rows, HD), jnp.float32)] * 3
        + [
            pltpu.VMEM((NX * NC, slab_rows, 2 * HD), jnp.float32),
            pltpu.SemaphoreType.DMA((3, NX * NZ)),
        ],
        compiler_params=pltpu.CompilerParams(vmem_limit_bytes=60 * 2**20),
        name="attend",
    )(
        lengths,
        queries,
        key_cache.reshape(rows * span, features),
        value_cache.reshape(rows * span, features),
        new_key,
        new_value,
        gate,
        up,
        down,
    )


def merge(arrived):
    f32 = jnp.float32
    part = arrived[:, :, :HD].astype(f32)
    info = arrived[:, :, HD : HD + 4].astype(f32)
    base_of = info[:, :, 0] + info[:, :, 1]
    factor = jnp.exp(base_of - jnp.max(base_of, axis=0, keepdims=True))
    whole = jnp.sum(factor * (info[:, :, 2] + info[:, :, 3]), axis=0)
    return jnp.sum((factor / whole)[..., None] * part, axis=0)


def expert_enter(state, gain, gate, up, pair):
    hidden, width = gate.shape
    return pl.pallas_call(
        enter_kernel,
        out_shape=jax.ShapeDtypeStruct((2 * NC, state.shape[1], HD), jnp.float32),
        in_specs=[VMEM] * 4 + [ANY],
        out_specs=VMEM,
        scratch_shapes=[
            pltpu.VMEM((2, hidden, width // NC), jnp.bfloat16),
            pltpu.SemaphoreType.DMA,
        ],
        compiler_params=pltpu.CompilerParams(vmem_limit_bytes=50 * 2**20),
        name="enter",
    )(state, gain, gate, up, pair)


def expert_leave(sums, down, pair):
    hidden, width = down.shape
    share = width // (NX * NZ * NC)
    return pl.pallas_call(
        leave_kernel,
        out_shape=jax.ShapeDtypeStruct((NX, NZ, sums.shape[2], share), jnp.bfloat16),
        in_specs=[VMEM] * 2 + [ANY],
        out_specs=VMEM,
        scratch_shapes=[
            pltpu.VMEM((hidden, width // NC), jnp.bfloat16),
            pltpu.SemaphoreType.DMA,
        ],
        compiler_params=pltpu.CompilerParams(vmem_limit_bytes=50 * 2**20),
        name="leave",
    )(sums, down, pair)


def body(
    queries,
    key_cache,
    value_cache,
    new_key,
    new_value,
    lengths,
    experts,
    combine,
    residual,
    norm_gain,
    w_gate,
    w_up,
    w_down,
):
    bf16, f32 = jnp.bfloat16, jnp.float32
    rows, width = residual.shape
    dev_count = NX * NZ * NC
    outer_count = lax.axis_size("zl") * lax.axis_size("y")
    copies = outer_count // EXPERTS
    at_x, at_z, at_c = (lax.axis_index(a) for a in DEV)
    share = width // dev_count
    own_heads = HEADS // dev_count
    slots = outer_count * CAP

    packet, others = local_attention(
        lengths,
        queries,
        key_cache,
        value_cache,
        new_key,
        new_value,
        w_gate.T,
        w_up.T,
        w_down,
    )

    pair = lax.all_gather(others, "c", axis=0, tiled=False)
    arrived = lax.all_to_all(packet, DEV, split_axis=0, concat_axis=0, tiled=True)
    attended = merge(arrived)
    attended = jnp.transpose(attended.reshape(NZ, own_heads, rows, HD), (2, 0, 1, 3))
    attended = attended.reshape(rows, NZ, share)
    res = residual.reshape(rows, NX, NZ, NC, share)
    res = lax.dynamic_slice(res, (0, at_x, 0, at_c, 0), (rows, 1, NZ, 1, share))
    state = res.reshape(rows, NZ, share).astype(f32) + attended
    own_state = lax.dynamic_index_in_dim(state, at_z, 1, keepdims=False)
    gain = norm_gain.reshape(NX, NZ, NC, share)
    gain = lax.dynamic_slice(gain, (at_x, 0, at_c, 0), (1, NZ, 1, share)).reshape(1, NZ, share)
    scaled = (state * gain).reshape(rows, NZ * share).astype(bf16)

    chosen = experts.reshape(rows * TOPK)
    hits = (chosen[:, None] == jnp.arange(EXPERTS, dtype=jnp.int32)[None, :]).astype(jnp.int32)
    rank = jnp.sum((jnp.cumsum(hits, axis=0) - hits) * hits, axis=1)
    slot = (rank[:, None] == jnp.arange(CAP, dtype=jnp.int32)[None, :]).astype(jnp.int32)
    placement = (hits[:, :, None] * slot[:, None, :]).reshape(rows, TOPK, EXPERTS, CAP)
    row_slots = jnp.sum(placement, axis=1)
    packed = jnp.einsum(
        "rec,rd->ecd", row_slots.astype(bf16), scaled, preferred_element_type=f32
    ).astype(bf16)
    outgoing = jnp.repeat(packed, copies, axis=0)
    incoming = lax.all_to_all(outgoing, OUTER, split_axis=0, concat_axis=0, tiled=True)
    slab = incoming.reshape(slots, NZ * share)
    over_x = lax.all_gather(slab, "x", axis=0, tiled=False)
    sums = expert_enter(over_x, norm_gain.reshape(1, width), w_gate.T, w_up.T, pair)
    sums = lax.all_gather(sums, "c", axis=0, tiled=False)
    cut = expert_leave(sums, w_down, pair)

    from_x = lax.all_to_all(cut, "x", split_axis=0, concat_axis=0, tiled=True)
    home = jnp.sum(from_x.astype(f32), axis=0).astype(bf16).reshape(NZ * outer_count, CAP, share)
    returned = lax.all_to_all(home, ("zh",) + OUTER, split_axis=0, concat_axis=0, tiled=True)
    returned = returned.reshape(NZ, EXPERTS, copies, CAP, share).astype(f32)
    expert_output = jnp.sum(returned, axis=(0, 2)).reshape(1, EXPERTS * CAP, share)
    mix_weights = jnp.sum(placement.astype(f32) * combine[:, :, None, None], axis=1)
    moe = jnp.sum(mix_weights.reshape(rows, EXPERTS * CAP, 1) * expert_output, axis=1)
    return (own_state + moe).astype(bf16)


def solution(mesh):
    fine = Mesh(mesh.devices.reshape(6, 8, NX, NZ, NC), OUTER + DEV)
    return jax.shard_map(
        body,
        mesh=fine,
        in_specs=(
            P(OUTER, None),
            P(OUTER, DEV, None),
            P(OUTER, DEV, None),
            P(OUTER, None),
            P(OUTER, None),
            P(OUTER),
            P(OUTER, None),
            P(OUTER, None),
            P(OUTER, None),
            P(),
            P(None, OUTER + DEV),
            P(None, OUTER + DEV),
            P(OUTER + DEV, None),
        ),
        out_specs=P(OUTER, DEV),
        check_vma=False,
    )
```

```python
import math

import jax
import jax.numpy as jnp
from jax import lax
from jax.experimental import pallas as pl
from jax.experimental.pallas import tpu as pltpu
from jax.sharding import Mesh
from jax.sharding import PartitionSpec as P

HEADS = 48
KVH = 8
HD = 128
EXPERTS = 8
TOPK = 2
CAP = 2
DEAD = -1e30

OUTER = ("zl", "y")
DEV = ("x", "zh", "c")
NX, NZ, NC = 4, 2, 2
ANY = pl.BlockSpec(memory_space=pl.ANY)
VMEM = pl.BlockSpec(memory_space=pltpu.VMEM)
NT = (((1,), (1,)), ((), ()))


def starts_of(core, share):
    return [pl.multiple_of((i * NC + core) * share, share) for i in range(NX * NZ)]


def pack_copies(refs, stage, sems):
    share = refs[0].shape[1] // (NX * NZ * NC)
    return [
        pltpu.make_async_copy(
            ref.at[:, pl.ds(start, share)],
            stage.at[kind, :, pl.ds(i * share, share)],
            sems.at[kind, i],
        )
        for kind, ref in enumerate(refs)
        for i, start in enumerate(starts_of(1 - lax.axis_index("c"), share))
    ]


def attend_kernel(
    length_ref,
    q_ref,
    k_ref,
    v_ref,
    nk_ref,
    nv_ref,
    gate_ref,
    up_ref,
    down_ref,
    out_ref,
    other_ref,
    q_rows,
    nk_rows,
    nv_rows,
    packed,
    stage,
    sems,
    out_sem,
):
    copies = pack_copies((gate_ref, up_ref, down_ref), stage, sems)
    for copy in copies:
        copy.start()
    f32, bf16 = jnp.float32, jnp.bfloat16
    tokens = q_ref.shape[0]
    span = k_ref.shape[0] // tokens
    group = HEADS // KVH
    lines = group * tokens
    half = lines // NC
    scale = 1.0 / math.sqrt(HD)
    dev_index = (lax.axis_index("x") * NZ + lax.axis_index("zh")) * NC + lax.axis_index("c")
    queries = q_ref[...].astype(f32)
    new_keys = nk_ref[...].astype(f32)
    new_values = nv_ref[...].astype(f32)
    for head in range(HEADS):
        g = head // group
        at = slice(head * tokens, (head + 1) * tokens)
        q_rows[at, :] = queries[:, head * HD : (head + 1) * HD]
        nk_rows[at, :] = new_keys[:, g * HD : (g + 1) * HD]
        nv_rows[at, :] = new_values[:, g * HD : (g + 1) * HD]
    all_lines = HEADS * tokens
    row = lax.broadcasted_iota(jnp.int32, (lines, tokens * span), 0) % tokens
    column = lax.broadcasted_iota(jnp.int32, (lines, tokens * span), 1)
    limit = jnp.zeros((lines, tokens * span), jnp.int32)
    for t in range(tokens):
        limit = jnp.where(row == t, length_ref[t], limit)
    live = (column // span == row) & (dev_index * span + column % span < limit)
    live = jnp.concatenate([live.astype(f32)] * KVH, axis=0) > 0.5
    lane = lax.broadcasted_iota(jnp.int32, (all_lines, HD), 1)
    first = dev_index == 0
    q = q_rows[...]
    scores = jnp.concatenate(
        [
            lax.dot_general(
                q[g * lines : (g + 1) * lines].astype(bf16),
                k_ref[:, g * HD : (g + 1) * HD],
                NT,
                preferred_element_type=f32,
            )
            for g in range(KVH)
        ],
        axis=0,
    )
    for copy in copies:
        copy.wait()
    leave = pltpu.make_async_copy(stage, other_ref, out_sem)
    leave.start()
    scores = jnp.where(live, scores * scale, DEAD)
    own = jnp.sum(q * nk_rows[...], axis=1, keepdims=True) * scale
    own = jnp.where(first, own, DEAD)
    top = jnp.maximum(jnp.max(scores, axis=1, keepdims=True), own)
    top_high = top.astype(bf16).astype(f32)
    top_low = (top - top_high).astype(bf16).astype(f32)
    base = top_high + top_low
    weights = jnp.where(live, jnp.exp(scores - base), 0.0).astype(bf16)
    own_weight = jnp.where(first, jnp.exp(own - base), 0.0).astype(bf16).astype(f32)
    acc = jnp.concatenate(
        [
            jnp.dot(
                weights[g * lines : (g + 1) * lines],
                v_ref[:, g * HD : (g + 1) * HD],
                preferred_element_type=f32,
            )
            for g in range(KVH)
        ],
        axis=0,
    )
    acc = acc + own_weight * nv_rows[...]
    total = jnp.sum(weights.astype(f32), axis=1, keepdims=True) + own_weight
    total_high = total.astype(bf16).astype(f32)
    total_low = total - total_high
    stats = jnp.where(
        lane == 0,
        top_high,
        jnp.where(lane == 1, top_low, jnp.where(lane == 2, total_high, total_low)),
    )
    for x in range(NX):
        for z in range(NZ):
            for c in range(NC):
                to = slice(z * half, (z + 1) * half)
                at = ((x * NZ + z) * NC + c) * half
                packed[x * NC + c, to, :HD] = acc[at : at + half]
                packed[x * NC + c, to, HD:] = stats[at : at + half]
    for x in range(NX):
        for c in range(NC):
            block = packed[x * NC + c].astype(bf16)
            for z in range(NZ):
                out_ref[(x * NZ + z) * NC + c] = block
    leave.wait()


def enter_kernel(state_ref, gain_ref, gate_ref, up_ref, other, out_ref):
    f32 = jnp.float32
    rows, span = state_ref.shape[1:]
    share = span // NZ
    hidden = gate_ref.shape[0]
    at_c = lax.axis_index("c")
    starts = starts_of(at_c, share)

    def columns(ref, x):
        return jnp.concatenate(
            [ref[:, pl.ds(s, share)] for s in starts[x * NZ : (x + 1) * NZ]], axis=1
        )

    squares = jnp.zeros((rows, HD), f32)
    own = [jnp.zeros((rows, hidden), f32)] * 2
    for x in range(NX):
        block = state_ref[x]
        for kind, ref in enumerate((gate_ref, up_ref)):
            own[kind] += lax.dot_general(block, columns(ref, x), NT, preferred_element_type=f32)
        state = block.astype(f32) / columns(gain_ref, x)
        state = state * state
        for at in range(0, span, HD):
            squares += state[:, at : at + HD]
    total = jnp.sum(squares, axis=1, keepdims=True)
    total = jnp.broadcast_to(total, (rows, HD - hidden))
    for kind in range(2):
        far = jnp.zeros((rows, hidden), f32)
        for x in range(NX):
            far += lax.dot_general(
                state_ref[x],
                other[kind, :, x * span : (x + 1) * span],
                NT,
                preferred_element_type=f32,
            )
        out_ref[kind * NC] = jnp.concatenate([own[kind], total], axis=1)
        out_ref[kind * NC + 1] = jnp.concatenate([far, total], axis=1)


def leave_kernel(sums_ref, down_ref, other, out_ref):
    f32, bf16 = jnp.float32, jnp.bfloat16
    hidden, width = down_ref.shape
    share = out_ref.shape[3]
    at_c = lax.axis_index("c")
    factor = None
    active = []
    for far in range(NC):
        gate = sums_ref[at_c, far] + sums_ref[1 - at_c, 1 - far]
        up = sums_ref[at_c, NC + far] + sums_ref[1 - at_c, NC + 1 - far]
        if factor is None:
            factor = lax.rsqrt(gate[:, HD - 1 :] / width + 1e-05)
        gate = gate[:, :hidden] * factor
        up = up[:, :hidden] * factor
        active.append((gate / (1.0 + jnp.exp(-gate)) * up).astype(bf16))
    for i, start in enumerate(starts_of(at_c, share)):
        near = jnp.dot(active[0], down_ref[:, pl.ds(start, share)], preferred_element_type=f32)
        far = jnp.dot(active[1], other[2, :, i * share : (i + 1) * share], preferred_element_type=f32)
        out_ref[i // NZ, i % NZ] = (near + far).astype(bf16)


def local_attention(lengths, queries, key_cache, value_cache, new_key, new_value, gate, up, down):
    rows, span, features = key_cache.shape
    slab_rows = HEADS // (NX * NC) * rows
    hidden, width = down.shape
    return pl.pallas_call(
        attend_kernel,
        out_shape=(
            jax.ShapeDtypeStruct((NX * NZ * NC, slab_rows, 2 * HD), jnp.bfloat16),
            jax.ShapeDtypeStruct((3, hidden, width // NC), jnp.bfloat16),
        ),
        in_specs=[pl.BlockSpec(memory_space=pltpu.SMEM)] + [pl.BlockSpec()] * 5 + [ANY] * 3,
        out_specs=(VMEM, ANY),
        scratch_shapes=[pltpu.VMEM((HEADS * rows, HD), jnp.float32)] * 3
        + [
            pltpu.VMEM((NX * NC, slab_rows, 2 * HD), jnp.float32),
            pltpu.VMEM((3, hidden, width // NC), jnp.bfloat16),
            pltpu.SemaphoreType.DMA((3, NX * NZ)),
            pltpu.SemaphoreType.DMA,
        ],
        compiler_params=pltpu.CompilerParams(vmem_limit_bytes=60 * 2**20),
        name="attend",
    )(
        lengths,
        queries,
        key_cache.reshape(rows * span, features),
        value_cache.reshape(rows * span, features),
        new_key,
        new_value,
        gate,
        up,
        down,
    )


def merge(arrived):
    f32 = jnp.float32
    part = arrived[:, :, :HD].astype(f32)
    info = arrived[:, :, HD : HD + 4].astype(f32)
    base_of = info[:, :, 0] + info[:, :, 1]
    factor = jnp.exp(base_of - jnp.max(base_of, axis=0, keepdims=True))
    whole = jnp.sum(factor * (info[:, :, 2] + info[:, :, 3]), axis=0)
    return jnp.sum((factor / whole)[..., None] * part, axis=0)


def expert_enter(state, gain, gate, up, other):
    return pl.pallas_call(
        enter_kernel,
        out_shape=jax.ShapeDtypeStruct((2 * NC, state.shape[1], HD), jnp.float32),
        in_specs=[VMEM] * 5,
        out_specs=VMEM,
        compiler_params=pltpu.CompilerParams(vmem_limit_bytes=16 * 2**20),
        name="enter",
    )(state, gain, gate, up, other)


def expert_leave(sums, down, other):
    share = down.shape[1] // (NX * NZ * NC)
    return pl.pallas_call(
        leave_kernel,
        out_shape=jax.ShapeDtypeStruct((NX, NZ, sums.shape[2], share), jnp.bfloat16),
        in_specs=[VMEM] * 3,
        out_specs=VMEM,
        compiler_params=pltpu.CompilerParams(vmem_limit_bytes=16 * 2**20),
        name="leave",
    )(sums, down, other)


def body(
    queries,
    key_cache,
    value_cache,
    new_key,
    new_value,
    lengths,
    experts,
    combine,
    residual,
    norm_gain,
    w_gate,
    w_up,
    w_down,
):
    bf16, f32 = jnp.bfloat16, jnp.float32
    rows, width = residual.shape
    dev_count = NX * NZ * NC
    outer_count = lax.axis_size("zl") * lax.axis_size("y")
    copies = outer_count // EXPERTS
    at_x, at_z, at_c = (lax.axis_index(a) for a in DEV)
    share = width // dev_count
    own_heads = HEADS // dev_count
    slots = outer_count * CAP

    packet, others = local_attention(
        lengths,
        queries,
        key_cache,
        value_cache,
        new_key,
        new_value,
        w_gate.T,
        w_up.T,
        w_down,
    )

    other = lax.ppermute(others, "c", [(0, 1), (1, 0)])
    arrived = lax.all_to_all(packet, DEV, split_axis=0, concat_axis=0, tiled=True)
    attended = merge(arrived)
    attended = jnp.transpose(attended.reshape(NZ, own_heads, rows, HD), (2, 0, 1, 3))
    attended = attended.reshape(rows, NZ, share)
    res = residual.reshape(rows, NX, NZ, NC, share)
    res = lax.dynamic_slice(res, (0, at_x, 0, at_c, 0), (rows, 1, NZ, 1, share))
    state = res.reshape(rows, NZ, share).astype(f32) + attended
    own_state = lax.dynamic_index_in_dim(state, at_z, 1, keepdims=False)
    gain = norm_gain.reshape(NX, NZ, NC, share)
    gain = lax.dynamic_slice(gain, (at_x, 0, at_c, 0), (1, NZ, 1, share)).reshape(1, NZ, share)
    scaled = (state * gain).reshape(rows, NZ * share).astype(bf16)

    chosen = experts.reshape(rows * TOPK)
    hits = (chosen[:, None] == jnp.arange(EXPERTS, dtype=jnp.int32)[None, :]).astype(jnp.int32)
    rank = jnp.sum((jnp.cumsum(hits, axis=0) - hits) * hits, axis=1)
    slot = (rank[:, None] == jnp.arange(CAP, dtype=jnp.int32)[None, :]).astype(jnp.int32)
    placement = (hits[:, :, None] * slot[:, None, :]).reshape(rows, TOPK, EXPERTS, CAP)
    row_slots = jnp.sum(placement, axis=1)
    packed = jnp.einsum(
        "rec,rd->ecd", row_slots.astype(bf16), scaled, preferred_element_type=f32
    ).astype(bf16)
    outgoing = jnp.repeat(packed, copies, axis=0)
    incoming = lax.all_to_all(outgoing, OUTER, split_axis=0, concat_axis=0, tiled=True)
    slab = incoming.reshape(slots, NZ * share)
    over_x = lax.all_gather(slab, "x", axis=0, tiled=False)
    sums = expert_enter(over_x, norm_gain.reshape(1, width), w_gate.T, w_up.T, other)
    sums = lax.all_gather(sums, "c", axis=0, tiled=False)
    cut = expert_leave(sums, w_down, other)

    from_x = lax.all_to_all(cut, "x", split_axis=0, concat_axis=0, tiled=True)
    home = jnp.sum(from_x.astype(f32), axis=0).astype(bf16).reshape(NZ * outer_count, CAP, share)
    returned = lax.all_to_all(home, ("zh",) + OUTER, split_axis=0, concat_axis=0, tiled=True)
    returned = returned.reshape(NZ, EXPERTS, copies, CAP, share).astype(f32)
    expert_output = jnp.sum(returned, axis=(0, 2)).reshape(1, EXPERTS * CAP, share)
    mix_weights = jnp.sum(placement.astype(f32) * combine[:, :, None, None], axis=1)
    moe = jnp.sum(mix_weights.reshape(rows, EXPERTS * CAP, 1) * expert_output, axis=1)
    return (own_state + moe).astype(bf16)


def solution(mesh):
    fine = Mesh(mesh.devices.reshape(6, 8, NX, NZ, NC), OUTER + DEV)
    return jax.shard_map(
        body,
        mesh=fine,
        in_specs=(
            P(OUTER, None),
            P(OUTER, DEV, None),
            P(OUTER, DEV, None),
            P(OUTER, None),
            P(OUTER, None),
            P(OUTER),
            P(OUTER, None),
            P(OUTER, None),
            P(OUTER, None),
            P(),
            P(None, OUTER + DEV),
            P(None, OUTER + DEV),
            P(OUTER + DEV, None),
        ),
        out_specs=P(OUTER, DEV),
        check_vma=False,
    )
```

```python
import math

import jax
import jax.numpy as jnp
from jax import lax
from jax.experimental import pallas as pl
from jax.experimental.pallas import tpu as pltpu
from jax.sharding import Mesh
from jax.sharding import PartitionSpec as P

HEADS = 48
KVH = 8
HD = 128
EXPERTS = 8
TOPK = 2
CAP = 2
DEAD = -1e30

OUTER = ("zl", "y")
DEV = ("x", "zh", "c")
NX, NZ, NC = 4, 2, 2
ANY = pl.BlockSpec(memory_space=pl.ANY)
VMEM = pl.BlockSpec(memory_space=pltpu.VMEM)
NT = (((1,), (1,)), ((), ()))


def starts_of(core, share):
    return [pl.multiple_of((i * NC + core) * share, share) for i in range(NX * NZ)]


def pack_kernel(gate_ref, up_ref, down_ref, own_ref, out_ref, sems):
    share = gate_ref.shape[1] // (NX * NZ * NC)
    at_c = lax.axis_index("c")
    refs = (gate_ref, up_ref, down_ref)
    copies = [
        pltpu.make_async_copy(
            refs[kind].at[:, pl.ds(start, share)],
            to.at[kind, :, pl.ds(i * share, share)],
            sems.at[side, kind, i],
        )
        for side, (to, core) in enumerate(((out_ref, 1 - at_c), (own_ref, at_c)))
        for kind in range(to.shape[0])
        for i, start in enumerate(starts_of(core, share))
    ]
    for copy in copies:
        copy.start()
    for copy in copies:
        copy.wait()


def attend_kernel(
    length_ref,
    q_ref,
    k_ref,
    v_ref,
    nk_ref,
    nv_ref,
    out_ref,
    q_rows,
    nk_rows,
    nv_rows,
    packed,
):
    f32, bf16 = jnp.float32, jnp.bfloat16
    tokens = q_ref.shape[0]
    span = k_ref.shape[0] // tokens
    group = HEADS // KVH
    lines = group * tokens
    half = lines // NC
    scale = 1.0 / math.sqrt(HD)
    dev_index = (lax.axis_index("x") * NZ + lax.axis_index("zh")) * NC + lax.axis_index("c")
    queries = q_ref[...].astype(f32)
    new_keys = nk_ref[...].astype(f32)
    new_values = nv_ref[...].astype(f32)
    for head in range(HEADS):
        g = head // group
        at = slice(head * tokens, (head + 1) * tokens)
        q_rows[at, :] = queries[:, head * HD : (head + 1) * HD]
        nk_rows[at, :] = new_keys[:, g * HD : (g + 1) * HD]
        nv_rows[at, :] = new_values[:, g * HD : (g + 1) * HD]
    all_lines = HEADS * tokens
    row = lax.broadcasted_iota(jnp.int32, (lines, tokens * span), 0) % tokens
    column = lax.broadcasted_iota(jnp.int32, (lines, tokens * span), 1)
    limit = jnp.zeros((lines, tokens * span), jnp.int32)
    for t in range(tokens):
        limit = jnp.where(row == t, length_ref[t], limit)
    live = (column // span == row) & (dev_index * span + column % span < limit)
    live = jnp.concatenate([live.astype(f32)] * KVH, axis=0) > 0.5
    lane = lax.broadcasted_iota(jnp.int32, (all_lines, HD), 1)
    first = dev_index == 0
    q = q_rows[...]
    scores = jnp.concatenate(
        [
            lax.dot_general(
                q[g * lines : (g + 1) * lines].astype(bf16),
                k_ref[:, g * HD : (g + 1) * HD],
                NT,
                preferred_element_type=f32,
            )
            for g in range(KVH)
        ],
        axis=0,
    )
    scores = jnp.where(live, scores * scale, DEAD)
    own = jnp.sum(q * nk_rows[...], axis=1, keepdims=True) * scale
    own = jnp.where(first, own, DEAD)
    top = jnp.maximum(jnp.max(scores, axis=1, keepdims=True), own)
    top_high = top.astype(bf16).astype(f32)
    top_low = (top - top_high).astype(bf16).astype(f32)
    base = top_high + top_low
    weights = jnp.where(live, jnp.exp(scores - base), 0.0).astype(bf16)
    own_weight = jnp.where(first, jnp.exp(own - base), 0.0).astype(bf16).astype(f32)
    acc = jnp.concatenate(
        [
            jnp.dot(
                weights[g * lines : (g + 1) * lines],
                v_ref[:, g * HD : (g + 1) * HD],
                preferred_element_type=f32,
            )
            for g in range(KVH)
        ],
        axis=0,
    )
    acc = acc + own_weight * nv_rows[...]
    total = jnp.sum(weights.astype(f32), axis=1, keepdims=True) + own_weight
    total_high = total.astype(bf16).astype(f32)
    total_low = total - total_high
    stats = jnp.where(
        lane == 0,
        top_high,
        jnp.where(lane == 1, top_low, jnp.where(lane == 2, total_high, total_low)),
    )
    for x in range(NX):
        for z in range(NZ):
            for c in range(NC):
                to = slice(z * half, (z + 1) * half)
                at = ((x * NZ + z) * NC + c) * half
                packed[x * NC + c, to, :HD] = acc[at : at + half]
                packed[x * NC + c, to, HD:] = stats[at : at + half]
    for x in range(NX):
        for c in range(NC):
            block = packed[x * NC + c].astype(bf16)
            for z in range(NZ):
                out_ref[(x * NZ + z) * NC + c] = block


def enter_kernel(state_ref, gain_ref, own, other, out_ref):
    f32 = jnp.float32
    rows, span = state_ref.shape[1:]
    share = span // NZ
    hidden = own.shape[1]
    starts = starts_of(lax.axis_index("c"), share)
    squares = jnp.zeros((rows, HD), f32)
    sums = [jnp.zeros((rows, hidden), f32)] * (2 * NC)
    for x in range(NX):
        block = state_ref[x]
        for kind in range(2):
            for far, ref in enumerate((own, other)):
                sums[kind * NC + far] += lax.dot_general(
                    block, ref[kind, :, x * span : (x + 1) * span], NT, preferred_element_type=f32
                )
        gain = [gain_ref[:, pl.ds(s, share)] for s in starts[x * NZ : (x + 1) * NZ]]
        state = block.astype(f32) / jnp.concatenate(gain, axis=1)
        state = state * state
        for at in range(0, span, HD):
            squares += state[:, at : at + HD]
    total = jnp.sum(squares, axis=1, keepdims=True)
    total = jnp.broadcast_to(total, (rows, HD - hidden))
    for i in range(2 * NC):
        out_ref[i] = jnp.concatenate([sums[i], total], axis=1)


def leave_kernel(sums_ref, down_ref, other, out_ref):
    f32, bf16 = jnp.float32, jnp.bfloat16
    hidden, width = down_ref.shape
    share = out_ref.shape[3]
    at_c = lax.axis_index("c")
    factor = None
    active = []
    for far in range(NC):
        gate = sums_ref[at_c, far] + sums_ref[1 - at_c, 1 - far]
        up = sums_ref[at_c, NC + far] + sums_ref[1 - at_c, NC + 1 - far]
        if factor is None:
            factor = lax.rsqrt(gate[:, HD - 1 :] / width + 1e-05)
        gate = gate[:, :hidden] * factor
        up = up[:, :hidden] * factor
        active.append((gate / (1.0 + jnp.exp(-gate)) * up).astype(bf16))
    for i, start in enumerate(starts_of(at_c, share)):
        near = jnp.dot(active[0], down_ref[:, pl.ds(start, share)], preferred_element_type=f32)
        far = jnp.dot(active[1], other[2, :, i * share : (i + 1) * share], preferred_element_type=f32)
        out_ref[i // NZ, i % NZ] = (near + far).astype(bf16)


def local_attention(lengths, queries, key_cache, value_cache, new_key, new_value):
    rows, span, features = key_cache.shape
    slab_rows = HEADS // (NX * NC) * rows
    return pl.pallas_call(
        attend_kernel,
        out_shape=jax.ShapeDtypeStruct((NX * NZ * NC, slab_rows, 2 * HD), jnp.bfloat16),
        in_specs=[pl.BlockSpec(memory_space=pltpu.SMEM)] + [pl.BlockSpec()] * 5,
        out_specs=VMEM,
        scratch_shapes=[pltpu.VMEM((HEADS * rows, HD), jnp.float32)] * 3
        + [pltpu.VMEM((NX * NC, slab_rows, 2 * HD), jnp.float32)],
        compiler_params=pltpu.CompilerParams(vmem_limit_bytes=60 * 2**20),
        name="attend",
    )(
        lengths,
        queries,
        key_cache.reshape(rows * span, features),
        value_cache.reshape(rows * span, features),
        new_key,
        new_value,
    )


def merge(arrived):
    f32 = jnp.float32
    part = arrived[:, :, :HD].astype(f32)
    info = arrived[:, :, HD : HD + 4].astype(f32)
    base_of = info[:, :, 0] + info[:, :, 1]
    factor = jnp.exp(base_of - jnp.max(base_of, axis=0, keepdims=True))
    whole = jnp.sum(factor * (info[:, :, 2] + info[:, :, 3]), axis=0)
    return jnp.sum((factor / whole)[..., None] * part, axis=0)


def pack_weights(gate, up, down):
    hidden, width = down.shape
    return pl.pallas_call(
        pack_kernel,
        out_shape=tuple(
            jax.ShapeDtypeStruct((kinds, hidden, width // NC), jnp.bfloat16) for kinds in (2, 3)
        ),
        in_specs=[ANY] * 3,
        out_specs=(VMEM, VMEM),
        scratch_shapes=[pltpu.SemaphoreType.DMA((2, 3, NX * NZ))],
        compiler_params=pltpu.CompilerParams(vmem_limit_bytes=60 * 2**20),
        name="pack",
    )(gate, up, down)


def expert_enter(state, gain, own, other):
    return pl.pallas_call(
        enter_kernel,
        out_shape=jax.ShapeDtypeStruct((2 * NC, state.shape[1], HD), jnp.float32),
        in_specs=[VMEM] * 4,
        out_specs=VMEM,
        compiler_params=pltpu.CompilerParams(vmem_limit_bytes=16 * 2**20),
        name="enter",
    )(state, gain, own, other)


def expert_leave(sums, down, other):
    share = down.shape[1] // (NX * NZ * NC)
    return pl.pallas_call(
        leave_kernel,
        out_shape=jax.ShapeDtypeStruct((NX, NZ, sums.shape[2], share), jnp.bfloat16),
        in_specs=[VMEM] * 3,
        out_specs=VMEM,
        compiler_params=pltpu.CompilerParams(vmem_limit_bytes=16 * 2**20),
        name="leave",
    )(sums, down, other)


def body(
    queries,
    key_cache,
    value_cache,
    new_key,
    new_value,
    lengths,
    experts,
    combine,
    residual,
    norm_gain,
    w_gate,
    w_up,
    w_down,
):
    bf16, f32 = jnp.bfloat16, jnp.float32
    rows, width = residual.shape
    dev_count = NX * NZ * NC
    outer_count = lax.axis_size("zl") * lax.axis_size("y")
    copies = outer_count // EXPERTS
    at_x, at_z, at_c = (lax.axis_index(a) for a in DEV)
    share = width // dev_count
    own_heads = HEADS // dev_count
    slots = outer_count * CAP

    packet = local_attention(lengths, queries, key_cache, value_cache, new_key, new_value)

    own, sent = pack_weights(w_gate.T, w_up.T, w_down)
    other = lax.ppermute(sent, "c", [(0, 1), (1, 0)])
    arrived = lax.all_to_all(packet, DEV, split_axis=0, concat_axis=0, tiled=True)
    attended = merge(arrived)
    attended = jnp.transpose(attended.reshape(NZ, own_heads, rows, HD), (2, 0, 1, 3))
    attended = attended.reshape(rows, NZ, share)
    res = residual.reshape(rows, NX, NZ, NC, share)
    res = lax.dynamic_slice(res, (0, at_x, 0, at_c, 0), (rows, 1, NZ, 1, share))
    state = res.reshape(rows, NZ, share).astype(f32) + attended
    own_state = lax.dynamic_index_in_dim(state, at_z, 1, keepdims=False)
    gain = norm_gain.reshape(NX, NZ, NC, share)
    gain = lax.dynamic_slice(gain, (at_x, 0, at_c, 0), (1, NZ, 1, share)).reshape(1, NZ, share)
    scaled = (state * gain).reshape(rows, NZ * share).astype(bf16)

    chosen = experts.reshape(rows * TOPK)
    hits = (chosen[:, None] == jnp.arange(EXPERTS, dtype=jnp.int32)[None, :]).astype(jnp.int32)
    rank = jnp.sum((jnp.cumsum(hits, axis=0) - hits) * hits, axis=1)
    slot = (rank[:, None] == jnp.arange(CAP, dtype=jnp.int32)[None, :]).astype(jnp.int32)
    placement = (hits[:, :, None] * slot[:, None, :]).reshape(rows, TOPK, EXPERTS, CAP)
    row_slots = jnp.sum(placement, axis=1)
    packed = jnp.einsum(
        "rec,rd->ecd", row_slots.astype(bf16), scaled, preferred_element_type=f32
    ).astype(bf16)
    outgoing = jnp.repeat(packed, copies, axis=0)
    incoming = lax.all_to_all(outgoing, OUTER, split_axis=0, concat_axis=0, tiled=True)
    slab = incoming.reshape(slots, NZ * share)
    over_x = lax.all_gather(slab, "x", axis=0, tiled=False)
    sums = expert_enter(over_x, norm_gain.reshape(1, width), own, other)
    sums = lax.all_gather(sums, "c", axis=0, tiled=False)
    cut = expert_leave(sums, w_down, other)

    from_x = lax.all_to_all(cut, "x", split_axis=0, concat_axis=0, tiled=True)
    home = jnp.sum(from_x.astype(f32), axis=0).astype(bf16).reshape(NZ * outer_count, CAP, share)
    returned = lax.all_to_all(home, ("zh",) + OUTER, split_axis=0, concat_axis=0, tiled=True)
    returned = returned.reshape(NZ, EXPERTS, copies, CAP, share).astype(f32)
    expert_output = jnp.sum(returned, axis=(0, 2)).reshape(1, EXPERTS * CAP, share)
    mix_weights = jnp.sum(placement.astype(f32) * combine[:, :, None, None], axis=1)
    moe = jnp.sum(mix_weights.reshape(rows, EXPERTS * CAP, 1) * expert_output, axis=1)
    return (own_state + moe).astype(bf16)


def solution(mesh):
    fine = Mesh(mesh.devices.reshape(6, 8, NX, NZ, NC), OUTER + DEV)
    return jax.shard_map(
        body,
        mesh=fine,
        in_specs=(
            P(OUTER, None),
            P(OUTER, DEV, None),
            P(OUTER, DEV, None),
            P(OUTER, None),
            P(OUTER, None),
            P(OUTER),
            P(OUTER, None),
            P(OUTER, None),
            P(OUTER, None),
            P(),
            P(None, OUTER + DEV),
            P(None, OUTER + DEV),
            P(OUTER + DEV, None),
        ),
        out_specs=P(OUTER, DEV),
        check_vma=False,
    )
```

```python
import math

import jax
import jax.numpy as jnp
from jax import lax
from jax.experimental import pallas as pl
from jax.experimental.pallas import tpu as pltpu
from jax.sharding import Mesh
from jax.sharding import PartitionSpec as P

HEADS = 48
KVH = 8
HD = 128
EXPERTS = 8
TOPK = 2
CAP = 2
DEAD = -1e30

OUTER = ("zl", "y")
DEV = ("x", "zh", "c")
NX, NZ, NC = 4, 2, 2
ANY = pl.BlockSpec(memory_space=pl.ANY)
VMEM = pl.BlockSpec(memory_space=pltpu.VMEM)
NT = (((1,), (1,)), ((), ()))


def starts_of(core, share):
    return [pl.multiple_of((i * NC + core) * share, share) for i in range(NX * NZ)]


def pack_kernel(gate_ref, up_ref, down_ref, own_ref, out_ref, stage, in_sems, out_sems):
    share = gate_ref.shape[1] // (NX * NZ * NC)
    at_c = lax.axis_index("c")
    refs = (gate_ref, up_ref, down_ref)
    groups = []
    for to, core in ((out_ref, 1 - at_c), (own_ref, at_c)):
        for kind in range(to.shape[0]):
            slot = len(groups)
            copies = [
                pltpu.make_async_copy(
                    refs[kind].at[:, pl.ds(start, share)],
                    stage.at[slot, :, pl.ds(i * share, share)],
                    in_sems.at[slot, i],
                )
                for i, start in enumerate(starts_of(core, share))
            ]
            groups.append(
                (copies, pltpu.make_async_copy(stage.at[slot], to.at[kind], out_sems.at[slot]))
            )
    for copies, _ in groups:
        for copy in copies:
            copy.start()
    for copies, leave in groups:
        for copy in copies:
            copy.wait()
        leave.start()
    for _, leave in groups:
        leave.wait()


def attend_kernel(
    length_ref,
    q_ref,
    k_ref,
    v_ref,
    nk_ref,
    nv_ref,
    out_ref,
    q_rows,
    nk_rows,
    nv_rows,
    packed,
):
    f32, bf16 = jnp.float32, jnp.bfloat16
    tokens = q_ref.shape[0]
    span = k_ref.shape[0] // tokens
    group = HEADS // KVH
    lines = group * tokens
    half = lines // NC
    scale = 1.0 / math.sqrt(HD)
    dev_index = (lax.axis_index("x") * NZ + lax.axis_index("zh")) * NC + lax.axis_index("c")
    queries = q_ref[...].astype(f32)
    new_keys = nk_ref[...].astype(f32)
    new_values = nv_ref[...].astype(f32)
    for head in range(HEADS):
        g = head // group
        at = slice(head * tokens, (head + 1) * tokens)
        q_rows[at, :] = queries[:, head * HD : (head + 1) * HD]
        nk_rows[at, :] = new_keys[:, g * HD : (g + 1) * HD]
        nv_rows[at, :] = new_values[:, g * HD : (g + 1) * HD]
    all_lines = HEADS * tokens
    row = lax.broadcasted_iota(jnp.int32, (lines, tokens * span), 0) % tokens
    column = lax.broadcasted_iota(jnp.int32, (lines, tokens * span), 1)
    limit = jnp.zeros((lines, tokens * span), jnp.int32)
    for t in range(tokens):
        limit = jnp.where(row == t, length_ref[t], limit)
    live = (column // span == row) & (dev_index * span + column % span < limit)
    live = jnp.concatenate([live.astype(f32)] * KVH, axis=0) > 0.5
    lane = lax.broadcasted_iota(jnp.int32, (all_lines, HD), 1)
    first = dev_index == 0
    q = q_rows[...]
    scores = jnp.concatenate(
        [
            lax.dot_general(
                q[g * lines : (g + 1) * lines].astype(bf16),
                k_ref[:, g * HD : (g + 1) * HD],
                NT,
                preferred_element_type=f32,
            )
            for g in range(KVH)
        ],
        axis=0,
    )
    scores = jnp.where(live, scores * scale, DEAD)
    own = jnp.sum(q * nk_rows[...], axis=1, keepdims=True) * scale
    own = jnp.where(first, own, DEAD)
    top = jnp.maximum(jnp.max(scores, axis=1, keepdims=True), own)
    top_high = top.astype(bf16).astype(f32)
    top_low = (top - top_high).astype(bf16).astype(f32)
    base = top_high + top_low
    weights = jnp.where(live, jnp.exp(scores - base), 0.0).astype(bf16)
    own_weight = jnp.where(first, jnp.exp(own - base), 0.0).astype(bf16).astype(f32)
    acc = jnp.concatenate(
        [
            jnp.dot(
                weights[g * lines : (g + 1) * lines],
                v_ref[:, g * HD : (g + 1) * HD],
                preferred_element_type=f32,
            )
            for g in range(KVH)
        ],
        axis=0,
    )
    acc = acc + own_weight * nv_rows[...]
    total = jnp.sum(weights.astype(f32), axis=1, keepdims=True) + own_weight
    total_high = total.astype(bf16).astype(f32)
    total_low = total - total_high
    stats = jnp.where(
        lane == 0,
        top_high,
        jnp.where(
            lane == 1,
            top_low,
            jnp.where(lane == 2, total_high, jnp.where(lane == 3, total_low, 0.0)),
        ),
    )
    for x in range(NX):
        for z in range(NZ):
            for c in range(NC):
                to = slice(z * half, (z + 1) * half)
                at = ((x * NZ + z) * NC + c) * half
                packed[x * NC + c, to, :HD] = acc[at : at + half]
                packed[x * NC + c, to, HD:] = stats[at : at + half]
    one_hot = lax.broadcasted_iota(jnp.int32, (lines, HD), 0) == lane[:lines]
    one_hot = one_hot.astype(f32).astype(bf16)
    for x in range(NX):
        for c in range(NC):
            block = packed[x * NC + c].astype(bf16)
            turned = lax.dot_general(
                block[:, HD:], one_hot, (((0,), (0,)), ((), ())), preferred_element_type=f32
            )
            block = jnp.concatenate([packed[x * NC + c, :, :HD], turned[:8]], axis=0).astype(bf16)
            for z in range(NZ):
                out_ref[(x * NZ + z) * NC + c] = block


def enter_kernel(state_ref, gain_ref, own, other, out_ref):
    f32 = jnp.float32
    rows, span = state_ref.shape[1:]
    share = span // NZ
    hidden = own.shape[1]
    starts = starts_of(lax.axis_index("c"), share)
    squares = jnp.zeros((rows, HD), f32)
    sums = [jnp.zeros((rows, hidden), f32)] * (2 * NC)
    for x in range(NX):
        block = state_ref[x]
        for kind in range(2):
            for far, ref in enumerate((own, other)):
                sums[kind * NC + far] += lax.dot_general(
                    block, ref[kind, :, x * span : (x + 1) * span], NT, preferred_element_type=f32
                )
        gain = [gain_ref[:, pl.ds(s, share)] for s in starts[x * NZ : (x + 1) * NZ]]
        state = block.astype(f32) / jnp.concatenate(gain, axis=1)
        state = state * state
        for at in range(0, span, HD):
            squares += state[:, at : at + HD]
    total = jnp.sum(squares, axis=1, keepdims=True)
    total = jnp.broadcast_to(total, (rows, HD - hidden))
    for i in range(2 * NC):
        out_ref[i] = jnp.concatenate([sums[i], total], axis=1)


def leave_kernel(sums_ref, down_ref, other, out_ref):
    f32, bf16 = jnp.float32, jnp.bfloat16
    hidden, width = down_ref.shape
    share = out_ref.shape[3]
    at_c = lax.axis_index("c")
    factor = None
    active = []
    for far in range(NC):
        gate = sums_ref[at_c, far] + sums_ref[1 - at_c, 1 - far]
        up = sums_ref[at_c, NC + far] + sums_ref[1 - at_c, NC + 1 - far]
        if factor is None:
            factor = lax.rsqrt(gate[:, HD - 1 :] / width + 1e-05)
        gate = gate[:, :hidden] * factor
        up = up[:, :hidden] * factor
        active.append((gate / (1.0 + jnp.exp(-gate)) * up).astype(bf16))
    for i, start in enumerate(starts_of(at_c, share)):
        near = jnp.dot(active[0], down_ref[:, pl.ds(start, share)], preferred_element_type=f32)
        far = jnp.dot(active[1], other[2, :, i * share : (i + 1) * share], preferred_element_type=f32)
        out_ref[i // NZ, i % NZ] = (near + far).astype(bf16)


def local_attention(lengths, queries, key_cache, value_cache, new_key, new_value):
    rows, span, features = key_cache.shape
    slab_rows = HEADS // (NX * NC) * rows
    return pl.pallas_call(
        attend_kernel,
        out_shape=jax.ShapeDtypeStruct((NX * NZ * NC, slab_rows + 8, HD), jnp.bfloat16),
        in_specs=[pl.BlockSpec(memory_space=pltpu.SMEM)] + [pl.BlockSpec()] * 5,
        out_specs=VMEM,
        scratch_shapes=[pltpu.VMEM((HEADS * rows, HD), jnp.float32)] * 3
        + [pltpu.VMEM((NX * NC, slab_rows, 2 * HD), jnp.float32)],
        compiler_params=pltpu.CompilerParams(vmem_limit_bytes=60 * 2**20),
        name="attend",
    )(
        lengths,
        queries,
        key_cache.reshape(rows * span, features),
        value_cache.reshape(rows * span, features),
        new_key,
        new_value,
    )


def merge(arrived):
    f32 = jnp.float32
    lines = arrived.shape[1] - 8
    part = arrived[:, :lines].astype(f32)
    info = arrived[:, lines : lines + 4, :lines].astype(f32)
    base_of = info[:, 0] + info[:, 1]
    factor = jnp.exp(base_of - jnp.max(base_of, axis=0, keepdims=True))
    whole = jnp.sum(factor * (info[:, 2] + info[:, 3]), axis=0)
    return jnp.sum((factor / whole)[..., None] * part, axis=0)


def pack_weights(gate, up, down):
    hidden, width = down.shape
    return pl.pallas_call(
        pack_kernel,
        out_shape=tuple(
            jax.ShapeDtypeStruct((kinds, hidden, width // NC), jnp.bfloat16) for kinds in (2, 3)
        ),
        in_specs=[ANY] * 3,
        out_specs=(ANY, ANY),
        scratch_shapes=[
            pltpu.VMEM((5, hidden, width // NC), jnp.bfloat16),
            pltpu.SemaphoreType.DMA((5, NX * NZ)),
            pltpu.SemaphoreType.DMA((5,)),
        ],
        compiler_params=pltpu.CompilerParams(vmem_limit_bytes=60 * 2**20),
        name="pack",
    )(gate, up, down)


def expert_enter(state, gain, own, other):
    return pl.pallas_call(
        enter_kernel,
        out_shape=jax.ShapeDtypeStruct((2 * NC, state.shape[1], HD), jnp.float32),
        in_specs=[VMEM] * 4,
        out_specs=VMEM,
        compiler_params=pltpu.CompilerParams(vmem_limit_bytes=16 * 2**20),
        name="enter",
    )(state, gain, own, other)


def expert_leave(sums, down, other):
    share = down.shape[1] // (NX * NZ * NC)
    return pl.pallas_call(
        leave_kernel,
        out_shape=jax.ShapeDtypeStruct((NX, NZ, sums.shape[2], share), jnp.bfloat16),
        in_specs=[VMEM] * 3,
        out_specs=VMEM,
        compiler_params=pltpu.CompilerParams(vmem_limit_bytes=16 * 2**20),
        name="leave",
    )(sums, down, other)


def body(
    queries,
    key_cache,
    value_cache,
    new_key,
    new_value,
    lengths,
    experts,
    combine,
    residual,
    norm_gain,
    w_gate,
    w_up,
    w_down,
):
    bf16, f32 = jnp.bfloat16, jnp.float32
    rows, width = residual.shape
    dev_count = NX * NZ * NC
    outer_count = lax.axis_size("zl") * lax.axis_size("y")
    copies = outer_count // EXPERTS
    at_x, at_z, at_c = (lax.axis_index(a) for a in DEV)
    share = width // dev_count
    own_heads = HEADS // dev_count
    slots = outer_count * CAP

    packet = local_attention(lengths, queries, key_cache, value_cache, new_key, new_value)

    own, sent = pack_weights(w_gate.T, w_up.T, w_down)
    other = lax.ppermute(sent, "c", [(0, 1), (1, 0)])
    arrived = lax.all_to_all(packet, DEV, split_axis=0, concat_axis=0, tiled=True)
    attended = merge(arrived)
    attended = jnp.transpose(attended.reshape(NZ, own_heads, rows, HD), (2, 0, 1, 3))
    attended = attended.reshape(rows, NZ, share)
    res = residual.reshape(rows, NX, NZ, NC, share)
    res = lax.dynamic_slice(res, (0, at_x, 0, at_c, 0), (rows, 1, NZ, 1, share))
    state = res.reshape(rows, NZ, share).astype(f32) + attended
    own_state = lax.dynamic_index_in_dim(state, at_z, 1, keepdims=False)
    gain = norm_gain.reshape(NX, NZ, NC, share)
    gain = lax.dynamic_slice(gain, (at_x, 0, at_c, 0), (1, NZ, 1, share)).reshape(1, NZ, share)
    scaled = (state * gain).reshape(rows, NZ * share).astype(bf16)

    chosen = experts.reshape(rows * TOPK)
    hits = (chosen[:, None] == jnp.arange(EXPERTS, dtype=jnp.int32)[None, :]).astype(jnp.int32)
    rank = jnp.sum((jnp.cumsum(hits, axis=0) - hits) * hits, axis=1)
    slot = (rank[:, None] == jnp.arange(CAP, dtype=jnp.int32)[None, :]).astype(jnp.int32)
    placement = (hits[:, :, None] * slot[:, None, :]).reshape(rows, TOPK, EXPERTS, CAP)
    row_slots = jnp.sum(placement, axis=1)
    packed = jnp.einsum(
        "rec,rd->ecd", row_slots.astype(bf16), scaled, preferred_element_type=f32
    ).astype(bf16)
    outgoing = jnp.repeat(packed, copies, axis=0)
    incoming = lax.all_to_all(outgoing, OUTER, split_axis=0, concat_axis=0, tiled=True)
    slab = incoming.reshape(slots, NZ * share)
    over_x = lax.all_gather(slab, "x", axis=0, tiled=False)
    sums = expert_enter(over_x, norm_gain.reshape(1, width), own, other)
    sums = lax.all_gather(sums, "c", axis=0, tiled=False)
    cut = expert_leave(sums, w_down, other)

    from_x = lax.all_to_all(cut, "x", split_axis=0, concat_axis=0, tiled=True)
    home = jnp.sum(from_x.astype(f32), axis=0).astype(bf16).reshape(NZ * outer_count, CAP, share)
    returned = lax.all_to_all(home, ("zh",) + OUTER, split_axis=0, concat_axis=0, tiled=True)
    returned = returned.reshape(NZ, EXPERTS, copies, CAP, share).astype(f32)
    expert_output = jnp.sum(returned, axis=(0, 2)).reshape(1, EXPERTS * CAP, share)
    mix_weights = jnp.sum(placement.astype(f32) * combine[:, :, None, None], axis=1)
    moe = jnp.sum(mix_weights.reshape(rows, EXPERTS * CAP, 1) * expert_output, axis=1)
    return (own_state + moe).astype(bf16)


def solution(mesh):
    fine = Mesh(mesh.devices.reshape(6, 8, NX, NZ, NC), OUTER + DEV)
    return jax.shard_map(
        body,
        mesh=fine,
        in_specs=(
            P(OUTER, None),
            P(OUTER, DEV, None),
            P(OUTER, DEV, None),
            P(OUTER, None),
            P(OUTER, None),
            P(OUTER),
            P(OUTER, None),
            P(OUTER, None),
            P(OUTER, None),
            P(),
            P(None, OUTER + DEV),
            P(None, OUTER + DEV),
            P(OUTER + DEV, None),
        ),
        out_specs=P(OUTER, DEV),
        check_vma=False,
    )
```

```python
import math

import jax
import jax.numpy as jnp
from jax import lax
from jax.experimental import pallas as pl
from jax.experimental.pallas import tpu as pltpu
from jax.sharding import Mesh
from jax.sharding import PartitionSpec as P

HEADS = 48
KVH = 8
HD = 128
EXPERTS = 8
TOPK = 2
CAP = 2
DEAD = -1e30

OUTER = ("zl", "y")
DEV = ("x", "zh", "c")
NX, NZ, NC = 4, 2, 2
ANY = pl.BlockSpec(memory_space=pl.ANY)
VMEM = pl.BlockSpec(memory_space=pltpu.VMEM)
NT = (((1,), (1,)), ((), ()))


def starts_of(core, share):
    return [pl.multiple_of((i * NC + core) * share, share) for i in range(NX * NZ)]


def pack_copies(refs, core, to, sems):
    share = refs[0].shape[1] // (NX * NZ * NC)
    return [
        [
            pltpu.make_async_copy(
                ref.at[:, pl.ds(start, share)],
                to.at[kind, :, pl.ds(i * share, share)],
                sems.at[kind, i],
            )
            for i, start in enumerate(starts_of(core, share))
        ]
        for kind, ref in enumerate(refs)
    ]


def pack_own_kernel(gate_ref, up_ref, out_ref, sems):
    groups = pack_copies((gate_ref, up_ref), lax.axis_index("c"), out_ref, sems)
    for copy in sum(groups, []):
        copy.start()
    for copy in sum(groups, []):
        copy.wait()


def pack_sent_kernel(gate_ref, up_ref, down_ref, out_ref, stage, in_sems, out_sems):
    other = 1 - lax.axis_index("c")
    groups = pack_copies((gate_ref, up_ref, down_ref), other, stage, in_sems)
    for copy in sum(groups, []):
        copy.start()
    leaves = []
    for kind, copies in enumerate(groups):
        for copy in copies:
            copy.wait()
        leaves.append(
            pltpu.make_async_copy(stage.at[kind], out_ref.at[kind], out_sems.at[kind])
        )
        leaves[-1].start()
    for leave in leaves:
        leave.wait()


def attend_kernel(
    length_ref,
    q_ref,
    k_ref,
    v_ref,
    nk_ref,
    nv_ref,
    out_ref,
    q_rows,
    nk_rows,
    nv_rows,
    packed,
):
    f32, bf16 = jnp.float32, jnp.bfloat16
    tokens = q_ref.shape[0]
    span = k_ref.shape[0] // tokens
    group = HEADS // KVH
    lines = group * tokens
    half = lines // NC
    scale = 1.0 / math.sqrt(HD)
    dev_index = (lax.axis_index("x") * NZ + lax.axis_index("zh")) * NC + lax.axis_index("c")
    queries = q_ref[...].astype(f32)
    new_keys = nk_ref[...].astype(f32)
    new_values = nv_ref[...].astype(f32)
    for head in range(HEADS):
        g = head // group
        at = slice(head * tokens, (head + 1) * tokens)
        q_rows[at, :] = queries[:, head * HD : (head + 1) * HD]
        nk_rows[at, :] = new_keys[:, g * HD : (g + 1) * HD]
        nv_rows[at, :] = new_values[:, g * HD : (g + 1) * HD]
    all_lines = HEADS * tokens
    row = lax.broadcasted_iota(jnp.int32, (lines, tokens * span), 0) % tokens
    column = lax.broadcasted_iota(jnp.int32, (lines, tokens * span), 1)
    limit = jnp.zeros((lines, tokens * span), jnp.int32)
    for t in range(tokens):
        limit = jnp.where(row == t, length_ref[t], limit)
    live = (column // span == row) & (dev_index * span + column % span < limit)
    live = jnp.concatenate([live.astype(f32)] * KVH, axis=0) > 0.5
    lane = lax.broadcasted_iota(jnp.int32, (all_lines, HD), 1)
    first = dev_index == 0
    q = q_rows[...]
    scores = jnp.concatenate(
        [
            lax.dot_general(
                q[g * lines : (g + 1) * lines].astype(bf16),
                k_ref[:, g * HD : (g + 1) * HD],
                NT,
                preferred_element_type=f32,
            )
            for g in range(KVH)
        ],
        axis=0,
    )
    scores = jnp.where(live, scores * scale, DEAD)
    own = jnp.sum(q * nk_rows[...], axis=1, keepdims=True) * scale
    own = jnp.where(first, own, DEAD)
    top = jnp.maximum(jnp.max(scores, axis=1, keepdims=True), own)
    top_high = top.astype(bf16).astype(f32)
    top_low = (top - top_high).astype(bf16).astype(f32)
    base = top_high + top_low
    weights = jnp.where(live, jnp.exp(scores - base), 0.0).astype(bf16)
    own_weight = jnp.where(first, jnp.exp(own - base), 0.0).astype(bf16).astype(f32)
    acc = jnp.concatenate(
        [
            jnp.dot(
                weights[g * lines : (g + 1) * lines],
                v_ref[:, g * HD : (g + 1) * HD],
                preferred_element_type=f32,
            )
            for g in range(KVH)
        ],
        axis=0,
    )
    acc = acc + own_weight * nv_rows[...]
    total = jnp.sum(weights.astype(f32), axis=1, keepdims=True) + own_weight
    total_high = total.astype(bf16).astype(f32)
    total_low = total - total_high
    stats = jnp.where(
        lane == 0,
        top_high,
        jnp.where(
            lane == 1,
            top_low,
            jnp.where(lane == 2, total_high, jnp.where(lane == 3, total_low, 0.0)),
        ),
    )
    for x in range(NX):
        for z in range(NZ):
            for c in range(NC):
                to = slice(z * half, (z + 1) * half)
                at = ((x * NZ + z) * NC + c) * half
                packed[x * NC + c, to, :HD] = acc[at : at + half]
                packed[x * NC + c, to, HD:] = stats[at : at + half]
    one_hot = lax.broadcasted_iota(jnp.int32, (lines, HD), 0) == lane[:lines]
    one_hot = one_hot.astype(f32).astype(bf16)
    for x in range(NX):
        for c in range(NC):
            block = packed[x * NC + c].astype(bf16)
            turned = lax.dot_general(
                block[:, HD:], one_hot, (((0,), (0,)), ((), ())), preferred_element_type=f32
            )
            block = jnp.concatenate([packed[x * NC + c, :, :HD], turned[:8]], axis=0).astype(bf16)
            for z in range(NZ):
                out_ref[(x * NZ + z) * NC + c] = block


def enter_kernel(state_ref, gain_ref, own, other, out_ref):
    f32 = jnp.float32
    rows, span = state_ref.shape[1:]
    share = span // NZ
    hidden = own.shape[1]
    starts = starts_of(lax.axis_index("c"), share)
    squares = jnp.zeros((rows, HD), f32)
    sums = [jnp.zeros((rows, hidden), f32)] * (2 * NC)
    for x in range(NX):
        block = state_ref[x]
        for kind in range(2):
            for far, ref in enumerate((own, other)):
                sums[kind * NC + far] += lax.dot_general(
                    block, ref[kind, :, x * span : (x + 1) * span], NT, preferred_element_type=f32
                )
        gain = [gain_ref[:, pl.ds(s, share)] for s in starts[x * NZ : (x + 1) * NZ]]
        state = block.astype(f32) / jnp.concatenate(gain, axis=1)
        state = state * state
        for at in range(0, span, HD):
            squares += state[:, at : at + HD]
    total = jnp.sum(squares, axis=1, keepdims=True)
    total = jnp.broadcast_to(total, (rows, HD - hidden))
    for i in range(2 * NC):
        out_ref[i] = jnp.concatenate([sums[i], total], axis=1)


def leave_kernel(sums_ref, down_ref, other, out_ref):
    f32, bf16 = jnp.float32, jnp.bfloat16
    hidden, width = down_ref.shape
    share = out_ref.shape[3]
    at_c = lax.axis_index("c")
    factor = None
    active = []
    for far in range(NC):
        gate = sums_ref[at_c, far] + sums_ref[1 - at_c, 1 - far]
        up = sums_ref[at_c, NC + far] + sums_ref[1 - at_c, NC + 1 - far]
        if factor is None:
            factor = lax.rsqrt(gate[:, HD - 1 :] / width + 1e-05)
        gate = gate[:, :hidden] * factor
        up = up[:, :hidden] * factor
        active.append((gate / (1.0 + jnp.exp(-gate)) * up).astype(bf16))
    for i, start in enumerate(starts_of(at_c, share)):
        near = jnp.dot(active[0], down_ref[:, pl.ds(start, share)], preferred_element_type=f32)
        far = jnp.dot(active[1], other[2, :, i * share : (i + 1) * share], preferred_element_type=f32)
        out_ref[i // NZ, i % NZ] = (near + far).astype(bf16)


def local_attention(lengths, queries, key_cache, value_cache, new_key, new_value):
    rows, span, features = key_cache.shape
    slab_rows = HEADS // (NX * NC) * rows
    return pl.pallas_call(
        attend_kernel,
        out_shape=jax.ShapeDtypeStruct((NX * NZ * NC, slab_rows + 8, HD), jnp.bfloat16),
        in_specs=[pl.BlockSpec(memory_space=pltpu.SMEM)] + [pl.BlockSpec()] * 5,
        out_specs=VMEM,
        scratch_shapes=[pltpu.VMEM((HEADS * rows, HD), jnp.float32)] * 3
        + [pltpu.VMEM((NX * NC, slab_rows, 2 * HD), jnp.float32)],
        compiler_params=pltpu.CompilerParams(vmem_limit_bytes=60 * 2**20),
        name="attend",
    )(
        lengths,
        queries,
        key_cache.reshape(rows * span, features),
        value_cache.reshape(rows * span, features),
        new_key,
        new_value,
    )


def merge(arrived):
    f32 = jnp.float32
    lines = arrived.shape[1] - 8
    part = arrived[:, :lines].astype(f32)
    info = arrived[:, lines : lines + 4, :lines].astype(f32)
    base_of = info[:, 0] + info[:, 1]
    factor = jnp.exp(base_of - jnp.max(base_of, axis=0, keepdims=True))
    whole = jnp.sum(factor * (info[:, 2] + info[:, 3]), axis=0)
    return jnp.sum((factor / whole)[..., None] * part, axis=0)


def pack_own(*weights):
    hidden, width = weights[0].shape
    packed = jax.ShapeDtypeStruct((len(weights), hidden, width // NC), jnp.bfloat16)
    return pl.pallas_call(
        pack_own_kernel,
        out_shape=packed,
        in_specs=[ANY] * len(weights),
        out_specs=VMEM,
        scratch_shapes=[pltpu.SemaphoreType.DMA((len(weights), NX * NZ))],
        compiler_params=pltpu.CompilerParams(vmem_limit_bytes=16 * 2**20),
        name="pack_own",
    )(*weights)


def pack_sent(*weights):
    hidden, width = weights[0].shape
    packed = jax.ShapeDtypeStruct((len(weights), hidden, width // NC), jnp.bfloat16)
    return pl.pallas_call(
        pack_sent_kernel,
        out_shape=packed,
        in_specs=[ANY] * len(weights),
        out_specs=ANY,
        scratch_shapes=[
            pltpu.VMEM(packed.shape, packed.dtype),
            pltpu.SemaphoreType.DMA((len(weights), NX * NZ)),
            pltpu.SemaphoreType.DMA((len(weights),)),
        ],
        compiler_params=pltpu.CompilerParams(vmem_limit_bytes=60 * 2**20),
        name="pack_sent",
    )(*weights)


def expert_enter(state, gain, own, other):
    return pl.pallas_call(
        enter_kernel,
        out_shape=jax.ShapeDtypeStruct((2 * NC, state.shape[1], HD), jnp.float32),
        in_specs=[VMEM] * 4,
        out_specs=VMEM,
        compiler_params=pltpu.CompilerParams(vmem_limit_bytes=16 * 2**20),
        name="enter",
    )(state, gain, own, other)


def expert_leave(sums, down, other):
    share = down.shape[1] // (NX * NZ * NC)
    return pl.pallas_call(
        leave_kernel,
        out_shape=jax.ShapeDtypeStruct((NX, NZ, sums.shape[2], share), jnp.bfloat16),
        in_specs=[VMEM] * 3,
        out_specs=VMEM,
        compiler_params=pltpu.CompilerParams(vmem_limit_bytes=16 * 2**20),
        name="leave",
    )(sums, down, other)


def body(
    queries,
    key_cache,
    value_cache,
    new_key,
    new_value,
    lengths,
    experts,
    combine,
    residual,
    norm_gain,
    w_gate,
    w_up,
    w_down,
):
    bf16, f32 = jnp.bfloat16, jnp.float32
    rows, width = residual.shape
    dev_count = NX * NZ * NC
    outer_count = lax.axis_size("zl") * lax.axis_size("y")
    copies = outer_count // EXPERTS
    at_x, at_z, at_c = (lax.axis_index(a) for a in DEV)
    share = width // dev_count
    own_heads = HEADS // dev_count
    slots = outer_count * CAP

    packet = local_attention(lengths, queries, key_cache, value_cache, new_key, new_value)

    sent = pack_sent(w_gate.T, w_up.T, w_down)
    other = lax.ppermute(sent, "c", [(0, 1), (1, 0)])
    arrived = lax.all_to_all(packet, DEV, split_axis=0, concat_axis=0, tiled=True)
    attended = merge(arrived)
    attended = jnp.transpose(attended.reshape(NZ, own_heads, rows, HD), (2, 0, 1, 3))
    attended = attended.reshape(rows, NZ, share)
    res = residual.reshape(rows, NX, NZ, NC, share)
    res = lax.dynamic_slice(res, (0, at_x, 0, at_c, 0), (rows, 1, NZ, 1, share))
    state = res.reshape(rows, NZ, share).astype(f32) + attended
    own_state = lax.dynamic_index_in_dim(state, at_z, 1, keepdims=False)
    gain = norm_gain.reshape(NX, NZ, NC, share)
    gain = lax.dynamic_slice(gain, (at_x, 0, at_c, 0), (1, NZ, 1, share)).reshape(1, NZ, share)
    scaled = (state * gain).reshape(rows, NZ * share).astype(bf16)

    chosen = experts.reshape(rows * TOPK)
    hits = (chosen[:, None] == jnp.arange(EXPERTS, dtype=jnp.int32)[None, :]).astype(jnp.int32)
    rank = jnp.sum((jnp.cumsum(hits, axis=0) - hits) * hits, axis=1)
    slot = (rank[:, None] == jnp.arange(CAP, dtype=jnp.int32)[None, :]).astype(jnp.int32)
    placement = (hits[:, :, None] * slot[:, None, :]).reshape(rows, TOPK, EXPERTS, CAP)
    row_slots = jnp.sum(placement, axis=1)
    packed = jnp.einsum(
        "rec,rd->ecd", row_slots.astype(bf16), scaled, preferred_element_type=f32
    ).astype(bf16)
    outgoing = jnp.repeat(packed, copies, axis=0)
    own = pack_own(w_gate.T, w_up.T)
    incoming = lax.all_to_all(outgoing, OUTER, split_axis=0, concat_axis=0, tiled=True)
    slab = incoming.reshape(slots, NZ * share)
    over_x = lax.all_gather(slab, "x", axis=0, tiled=False)
    sums = expert_enter(over_x, norm_gain.reshape(1, width), own, other)
    sums = lax.all_gather(sums, "c", axis=0, tiled=False)
    cut = expert_leave(sums, w_down, other)

    from_x = lax.all_to_all(cut, "x", split_axis=0, concat_axis=0, tiled=True)
    home = jnp.sum(from_x.astype(f32), axis=0).astype(bf16).reshape(NZ * outer_count, CAP, share)
    returned = lax.all_to_all(home, ("zh",) + OUTER, split_axis=0, concat_axis=0, tiled=True)
    returned = returned.reshape(NZ, EXPERTS, copies, CAP, share).astype(f32)
    expert_output = jnp.sum(returned, axis=(0, 2)).reshape(1, EXPERTS * CAP, share)
    mix_weights = jnp.sum(placement.astype(f32) * combine[:, :, None, None], axis=1)
    moe = jnp.sum(mix_weights.reshape(rows, EXPERTS * CAP, 1) * expert_output, axis=1)
    return (own_state + moe).astype(bf16)


def solution(mesh):
    fine = Mesh(mesh.devices.reshape(6, 8, NX, NZ, NC), OUTER + DEV)
    return jax.shard_map(
        body,
        mesh=fine,
        in_specs=(
            P(OUTER, None),
            P(OUTER, DEV, None),
            P(OUTER, DEV, None),
            P(OUTER, None),
            P(OUTER, None),
            P(OUTER),
            P(OUTER, None),
            P(OUTER, None),
            P(OUTER, None),
            P(),
            P(None, OUTER + DEV),
            P(None, OUTER + DEV),
            P(OUTER + DEV, None),
        ),
        out_specs=P(OUTER, DEV),
        check_vma=False,
    )
```

```python
import math

import jax
import jax.numpy as jnp
from jax import lax
from jax.experimental import pallas as pl
from jax.experimental.pallas import tpu as pltpu
from jax.sharding import Mesh
from jax.sharding import PartitionSpec as P

HEADS = 48
KVH = 8
HD = 128
EXPERTS = 8
TOPK = 2
CAP = 2
DEAD = -1e30

OUTER = ("zl", "y")
DEV = ("x", "zh", "c")
NX, NZ, NC = 4, 2, 2
ANY = pl.BlockSpec(memory_space=pl.ANY)
VMEM = pl.BlockSpec(memory_space=pltpu.VMEM)
NT = (((1,), (1,)), ((), ()))


def starts_of(core, share):
    return [pl.multiple_of((i * NC + core) * share, share) for i in range(NX * NZ)]


def pack_kernel(
    gate_ref,
    up_ref,
    down_ref,
    experts_ref,
    combine_ref,
    own_ref,
    out_ref,
    place_ref,
    mix_ref,
    stage,
    experts,
    combine,
    in_sems,
    out_sems,
    small_sems,
):
    share = gate_ref.shape[1] // (NX * NZ * NC)
    at_c = lax.axis_index("c")
    refs = (gate_ref, up_ref, down_ref)
    groups = []
    for to, core in ((out_ref, 1 - at_c), (own_ref, at_c)):
        for kind in range(to.shape[0]):
            slot = len(groups)
            copies = [
                pltpu.make_async_copy(
                    refs[kind].at[:, pl.ds(start, share)],
                    stage.at[slot, :, pl.ds(i * share, share)],
                    in_sems.at[slot, i],
                )
                for i, start in enumerate(starts_of(core, share))
            ]
            groups.append(
                (copies, pltpu.make_async_copy(stage.at[slot], to.at[kind], out_sems.at[slot]))
            )
    small = [
        pltpu.make_async_copy(experts_ref, experts, small_sems.at[0]),
        pltpu.make_async_copy(combine_ref, combine, small_sems.at[1]),
    ]
    for copy in small:
        copy.start()
    for copies, _ in groups:
        for copy in copies:
            copy.start()

    for copy in small:
        copy.wait()
    choices = [(r, k) for r in range(place_ref.shape[0]) for k in range(TOPK)]
    chosen = [experts[k, r] for r, k in choices]
    row = lax.broadcasted_iota(jnp.int32, place_ref.shape, 0)
    column = lax.broadcasted_iota(jnp.int32, place_ref.shape, 1)
    place = jnp.zeros(place_ref.shape, jnp.float32)
    mix = jnp.zeros(place_ref.shape, jnp.float32)
    for i, (r, k) in enumerate(choices):
        rank = jnp.int32(0)
        for earlier in chosen[:i]:
            rank += jnp.where(earlier == chosen[i], 1, 0)
        hit = (row == r) & (column == chosen[i] * CAP + rank)
        place = jnp.where(hit, 1.0, place)
        mix = jnp.where(hit, combine[k, r], mix)
    place_ref[...] = place
    mix_ref[...] = mix

    for copies, leave in groups:
        for copy in copies:
            copy.wait()
        leave.start()
    for _, leave in groups:
        leave.wait()


def attend_kernel(
    length_ref,
    q_ref,
    k_ref,
    v_ref,
    nk_ref,
    nv_ref,
    out_ref,
    q_rows,
    nk_rows,
    nv_rows,
    packed,
):
    f32, bf16 = jnp.float32, jnp.bfloat16
    tokens = q_ref.shape[0]
    span = k_ref.shape[0] // tokens
    group = HEADS // KVH
    lines = group * tokens
    half = lines // NC
    scale = 1.0 / math.sqrt(HD)
    dev_index = (lax.axis_index("x") * NZ + lax.axis_index("zh")) * NC + lax.axis_index("c")
    queries = q_ref[...].astype(f32)
    new_keys = nk_ref[...].astype(f32)
    new_values = nv_ref[...].astype(f32)
    for head in range(HEADS):
        g = head // group
        at = slice(head * tokens, (head + 1) * tokens)
        q_rows[at, :] = queries[:, head * HD : (head + 1) * HD]
        nk_rows[at, :] = new_keys[:, g * HD : (g + 1) * HD]
        nv_rows[at, :] = new_values[:, g * HD : (g + 1) * HD]
    all_lines = HEADS * tokens
    row = lax.broadcasted_iota(jnp.int32, (lines, tokens * span), 0) % tokens
    column = lax.broadcasted_iota(jnp.int32, (lines, tokens * span), 1)
    limit = jnp.zeros((lines, tokens * span), jnp.int32)
    for t in range(tokens):
        limit = jnp.where(row == t, length_ref[t], limit)
    live = (column // span == row) & (dev_index * span + column % span < limit)
    live = jnp.concatenate([live.astype(f32)] * KVH, axis=0) > 0.5
    lane = lax.broadcasted_iota(jnp.int32, (all_lines, HD), 1)
    first = dev_index == 0
    q = q_rows[...]
    scores = jnp.concatenate(
        [
            lax.dot_general(
                q[g * lines : (g + 1) * lines].astype(bf16),
                k_ref[:, g * HD : (g + 1) * HD],
                NT,
                preferred_element_type=f32,
            )
            for g in range(KVH)
        ],
        axis=0,
    )
    scores = jnp.where(live, scores * scale, DEAD)
    own = jnp.sum(q * nk_rows[...], axis=1, keepdims=True) * scale
    own = jnp.where(first, own, DEAD)
    top = jnp.maximum(jnp.max(scores, axis=1, keepdims=True), own)
    top_high = top.astype(bf16).astype(f32)
    top_low = (top - top_high).astype(bf16).astype(f32)
    base = top_high + top_low
    weights = jnp.where(live, jnp.exp(scores - base), 0.0).astype(bf16)
    own_weight = jnp.where(first, jnp.exp(own - base), 0.0).astype(bf16).astype(f32)
    acc = jnp.concatenate(
        [
            jnp.dot(
                weights[g * lines : (g + 1) * lines],
                v_ref[:, g * HD : (g + 1) * HD],
                preferred_element_type=f32,
            )
            for g in range(KVH)
        ],
        axis=0,
    )
    acc = acc + own_weight * nv_rows[...]
    total = jnp.sum(weights.astype(f32), axis=1, keepdims=True) + own_weight
    total_high = total.astype(bf16).astype(f32)
    total_low = total - total_high
    stats = jnp.where(
        lane == 0,
        top_high,
        jnp.where(
            lane == 1,
            top_low,
            jnp.where(lane == 2, total_high, jnp.where(lane == 3, total_low, 0.0)),
        ),
    )
    for x in range(NX):
        for z in range(NZ):
            for c in range(NC):
                to = slice(z * half, (z + 1) * half)
                at = ((x * NZ + z) * NC + c) * half
                packed[x * NC + c, to, :HD] = acc[at : at + half]
                packed[x * NC + c, to, HD:] = stats[at : at + half]
    one_hot = lax.broadcasted_iota(jnp.int32, (lines, HD), 0) == lane[:lines]
    one_hot = one_hot.astype(f32).astype(bf16)
    for x in range(NX):
        for c in range(NC):
            block = packed[x * NC + c].astype(bf16)
            turned = lax.dot_general(
                block[:, HD:], one_hot, (((0,), (0,)), ((), ())), preferred_element_type=f32
            )
            block = jnp.concatenate([packed[x * NC + c, :, :HD], turned[:8]], axis=0).astype(bf16)
            for z in range(NZ):
                out_ref[(x * NZ + z) * NC + c] = block


def enter_kernel(state_ref, gain_ref, own, other, out_ref):
    f32 = jnp.float32
    rows, span = state_ref.shape[1:]
    share = span // NZ
    hidden = own.shape[1]
    starts = starts_of(lax.axis_index("c"), share)
    squares = jnp.zeros((rows, HD), f32)
    sums = [jnp.zeros((rows, hidden), f32)] * (2 * NC)
    for x in range(NX):
        block = state_ref[x]
        for kind in range(2):
            for far, ref in enumerate((own, other)):
                sums[kind * NC + far] += lax.dot_general(
                    block, ref[kind, :, x * span : (x + 1) * span], NT, preferred_element_type=f32
                )
        gain = [gain_ref[:, pl.ds(s, share)] for s in starts[x * NZ : (x + 1) * NZ]]
        state = block.astype(f32) / jnp.concatenate(gain, axis=1)
        state = state * state
        for at in range(0, span, HD):
            squares += state[:, at : at + HD]
    total = jnp.sum(squares, axis=1, keepdims=True)
    total = jnp.broadcast_to(total, (rows, HD - hidden))
    for i in range(2 * NC):
        out_ref[i] = jnp.concatenate([sums[i], total], axis=1)


def leave_kernel(sums_ref, down_ref, other, out_ref):
    f32, bf16 = jnp.float32, jnp.bfloat16
    hidden, width = down_ref.shape
    share = out_ref.shape[3]
    at_c = lax.axis_index("c")
    factor = None
    active = []
    for far in range(NC):
        gate = sums_ref[at_c, far] + sums_ref[1 - at_c, 1 - far]
        up = sums_ref[at_c, NC + far] + sums_ref[1 - at_c, NC + 1 - far]
        if factor is None:
            factor = lax.rsqrt(gate[:, HD - 1 :] / width + 1e-05)
        gate = gate[:, :hidden] * factor
        up = up[:, :hidden] * factor
        active.append((gate / (1.0 + jnp.exp(-gate)) * up).astype(bf16))
    for i, start in enumerate(starts_of(at_c, share)):
        near = jnp.dot(active[0], down_ref[:, pl.ds(start, share)], preferred_element_type=f32)
        far = jnp.dot(active[1], other[2, :, i * share : (i + 1) * share], preferred_element_type=f32)
        out_ref[i // NZ, i % NZ] = (near + far).astype(bf16)


def local_attention(lengths, queries, key_cache, value_cache, new_key, new_value):
    rows, span, features = key_cache.shape
    slab_rows = HEADS // (NX * NC) * rows
    return pl.pallas_call(
        attend_kernel,
        out_shape=jax.ShapeDtypeStruct((NX * NZ * NC, slab_rows + 8, HD), jnp.bfloat16),
        in_specs=[pl.BlockSpec(memory_space=pltpu.SMEM)] + [pl.BlockSpec()] * 5,
        out_specs=VMEM,
        scratch_shapes=[pltpu.VMEM((HEADS * rows, HD), jnp.float32)] * 3
        + [pltpu.VMEM((NX * NC, slab_rows, 2 * HD), jnp.float32)],
        compiler_params=pltpu.CompilerParams(vmem_limit_bytes=60 * 2**20),
        name="attend",
    )(
        lengths,
        queries,
        key_cache.reshape(rows * span, features),
        value_cache.reshape(rows * span, features),
        new_key,
        new_value,
    )


def merge(arrived):
    f32 = jnp.float32
    lines = arrived.shape[1] - 8
    part = arrived[:, :lines].astype(f32)
    info = arrived[:, lines : lines + 4, :lines].astype(f32)
    base_of = info[:, 0] + info[:, 1]
    factor = jnp.exp(base_of - jnp.max(base_of, axis=0, keepdims=True))
    whole = jnp.sum(factor * (info[:, 2] + info[:, 3]), axis=0)
    return jnp.sum((factor / whole)[..., None] * part, axis=0)


def pack_weights(gate, up, down, experts, combine):
    rows = experts.shape[1]
    slots = jax.ShapeDtypeStruct((rows, EXPERTS * CAP), jnp.float32)
    hidden, width = down.shape
    return pl.pallas_call(
        pack_kernel,
        out_shape=tuple(
            jax.ShapeDtypeStruct((kinds, hidden, width // NC), jnp.bfloat16) for kinds in (2, 3)
        )
        + (slots, slots),
        in_specs=[ANY] * 5,
        out_specs=(ANY, ANY, VMEM, VMEM),
        scratch_shapes=[
            pltpu.VMEM((5, hidden, width // NC), jnp.bfloat16),
            pltpu.SMEM(experts.shape, jnp.int32),
            pltpu.SMEM(combine.shape, jnp.float32),
            pltpu.SemaphoreType.DMA((5, NX * NZ)),
            pltpu.SemaphoreType.DMA((5,)),
            pltpu.SemaphoreType.DMA((2,)),
        ],
        compiler_params=pltpu.CompilerParams(vmem_limit_bytes=60 * 2**20),
        name="pack",
    )(gate, up, down, experts, combine)


def expert_enter(state, gain, own, other):
    return pl.pallas_call(
        enter_kernel,
        out_shape=jax.ShapeDtypeStruct((2 * NC, state.shape[1], HD), jnp.float32),
        in_specs=[VMEM] * 4,
        out_specs=VMEM,
        compiler_params=pltpu.CompilerParams(vmem_limit_bytes=16 * 2**20),
        name="enter",
    )(state, gain, own, other)


def expert_leave(sums, down, other):
    share = down.shape[1] // (NX * NZ * NC)
    return pl.pallas_call(
        leave_kernel,
        out_shape=jax.ShapeDtypeStruct((NX, NZ, sums.shape[2], share), jnp.bfloat16),
        in_specs=[VMEM] * 3,
        out_specs=VMEM,
        compiler_params=pltpu.CompilerParams(vmem_limit_bytes=16 * 2**20),
        name="leave",
    )(sums, down, other)


def body(
    queries,
    key_cache,
    value_cache,
    new_key,
    new_value,
    lengths,
    experts,
    combine,
    residual,
    norm_gain,
    w_gate,
    w_up,
    w_down,
):
    bf16, f32 = jnp.bfloat16, jnp.float32
    rows, width = residual.shape
    dev_count = NX * NZ * NC
    outer_count = lax.axis_size("zl") * lax.axis_size("y")
    copies = outer_count // EXPERTS
    at_x, at_z, at_c = (lax.axis_index(a) for a in DEV)
    share = width // dev_count
    own_heads = HEADS // dev_count
    slots = outer_count * CAP

    packet = local_attention(lengths, queries, key_cache, value_cache, new_key, new_value)

    own, sent, place, mix = pack_weights(w_gate.T, w_up.T, w_down, experts.T, combine.T)
    other = lax.ppermute(sent, "c", [(0, 1), (1, 0)])
    arrived = lax.all_to_all(packet, DEV, split_axis=0, concat_axis=0, tiled=True)
    attended = merge(arrived)
    attended = jnp.transpose(attended.reshape(NZ, own_heads, rows, HD), (2, 0, 1, 3))
    attended = attended.reshape(rows, NZ, share)
    res = residual.reshape(rows, NX, NZ, NC, share)
    res = lax.dynamic_slice(res, (0, at_x, 0, at_c, 0), (rows, 1, NZ, 1, share))
    state = res.reshape(rows, NZ, share).astype(f32) + attended
    own_state = lax.dynamic_index_in_dim(state, at_z, 1, keepdims=False)
    gain = norm_gain.reshape(NX, NZ, NC, share)
    gain = lax.dynamic_slice(gain, (at_x, 0, at_c, 0), (1, NZ, 1, share)).reshape(1, NZ, share)
    scaled = (state * gain).reshape(rows, NZ * share).astype(bf16)

    packed = jnp.einsum(
        "rs,rd->sd", place.astype(bf16), scaled, preferred_element_type=f32
    ).astype(bf16)
    packed = packed.reshape(EXPERTS, CAP, NZ * share)
    outgoing = jnp.repeat(packed, copies, axis=0)
    outgoing, own_state = lax.optimization_barrier((outgoing, own_state))
    incoming = lax.all_to_all(outgoing, OUTER, split_axis=0, concat_axis=0, tiled=True)
    slab = incoming.reshape(slots, NZ * share)
    over_x = lax.all_gather(slab, "x", axis=0, tiled=False)
    sums = expert_enter(over_x, norm_gain.reshape(1, width), own, other)
    sums = lax.all_gather(sums, "c", axis=0, tiled=False)
    cut = expert_leave(sums, w_down, other)

    from_x = lax.all_to_all(cut, "x", split_axis=0, concat_axis=0, tiled=True)
    home = jnp.sum(from_x.astype(f32), axis=0).astype(bf16).reshape(NZ * outer_count, CAP, share)
    returned = lax.all_to_all(home, ("zh",) + OUTER, split_axis=0, concat_axis=0, tiled=True)
    returned = returned.reshape(NZ, EXPERTS, copies, CAP, share).astype(f32)
    expert_output = jnp.sum(returned, axis=(0, 2)).reshape(1, EXPERTS * CAP, share)
    moe = jnp.sum(mix.reshape(rows, EXPERTS * CAP, 1) * expert_output, axis=1)
    return (own_state + moe).astype(bf16)


def solution(mesh):
    fine = Mesh(mesh.devices.reshape(6, 8, NX, NZ, NC), OUTER + DEV)
    return jax.shard_map(
        body,
        mesh=fine,
        in_specs=(
            P(OUTER, None),
            P(OUTER, DEV, None),
            P(OUTER, DEV, None),
            P(OUTER, None),
            P(OUTER, None),
            P(OUTER),
            P(OUTER, None),
            P(OUTER, None),
            P(OUTER, None),
            P(),
            P(None, OUTER + DEV),
            P(None, OUTER + DEV),
            P(OUTER + DEV, None),
        ),
        out_specs=P(OUTER, DEV),
        check_vma=False,
    )
```

```python
import math

import jax
import jax.numpy as jnp
from jax import lax
from jax.experimental import pallas as pl
from jax.experimental.pallas import tpu as pltpu
from jax.sharding import Mesh
from jax.sharding import PartitionSpec as P

HEADS = 48
KVH = 8
HD = 128
EXPERTS = 8
TOPK = 2
CAP = 2
DEAD = -1e30

OUTER = ("zl", "y")
DEV = ("x", "zh", "c")
NX, NZ, NC = 4, 2, 2
ANY = pl.BlockSpec(memory_space=pl.ANY)
VMEM = pl.BlockSpec(memory_space=pltpu.VMEM)
NT = (((1,), (1,)), ((), ()))


def starts_of(core, share):
    return [pl.multiple_of((i * NC + core) * share, share) for i in range(NX * NZ)]


def pack_kernel(
    gate_ref,
    up_ref,
    down_ref,
    experts_ref,
    combine_ref,
    own_ref,
    out_ref,
    place_ref,
    mix_ref,
    stage,
    experts,
    combine,
    in_sems,
    out_sems,
    small_sems,
):
    share = gate_ref.shape[1] // (NX * NZ * NC)
    at_c = lax.axis_index("c")
    refs = (gate_ref, up_ref, down_ref)
    groups = []
    for to, core in ((out_ref, 1 - at_c), (own_ref, at_c)):
        for kind in range(to.shape[0]):
            slot = len(groups)
            copies = [
                pltpu.make_async_copy(
                    refs[kind].at[:, pl.ds(start, share)],
                    stage.at[slot, :, pl.ds(i * share, share)],
                    in_sems.at[slot, i],
                )
                for i, start in enumerate(starts_of(core, share))
            ]
            groups.append(
                (copies, pltpu.make_async_copy(stage.at[slot], to.at[kind], out_sems.at[slot]))
            )
    for copies, _ in groups:
        for copy in copies:
            copy.start()
    small = [
        pltpu.make_async_copy(experts_ref, experts, small_sems.at[0]),
        pltpu.make_async_copy(combine_ref, combine, small_sems.at[1]),
    ]
    for copy in small:
        copy.start()

    for copies, leave in groups:
        for copy in copies:
            copy.wait()
        leave.start()

    for copy in small:
        copy.wait()
    choices = [(r, k) for r in range(place_ref.shape[0]) for k in range(TOPK)]
    chosen = [experts[k, r] for r, k in choices]
    row = lax.broadcasted_iota(jnp.int32, place_ref.shape, 0)
    column = lax.broadcasted_iota(jnp.int32, place_ref.shape, 1)
    place = jnp.zeros(place_ref.shape, jnp.float32)
    mix = jnp.zeros(place_ref.shape, jnp.float32)
    for i, (r, k) in enumerate(choices):
        rank = jnp.int32(0)
        for earlier in chosen[:i]:
            rank += jnp.where(earlier == chosen[i], 1, 0)
        hit = (row == r) & (column == chosen[i] * CAP + rank)
        place = jnp.where(hit, 1.0, place)
        mix = jnp.where(hit, combine[k, r], mix)
    place_ref[...] = place
    mix_ref[...] = mix

    for _, leave in groups:
        leave.wait()


def attend_kernel(
    length_ref,
    q_ref,
    k_ref,
    v_ref,
    nk_ref,
    nv_ref,
    out_ref,
    q_rows,
    nk_rows,
    nv_rows,
    packed,
):
    f32, bf16 = jnp.float32, jnp.bfloat16
    tokens = q_ref.shape[0]
    span = k_ref.shape[0] // tokens
    group = HEADS // KVH
    lines = group * tokens
    half = lines // NC
    scale = 1.0 / math.sqrt(HD)
    dev_index = (lax.axis_index("x") * NZ + lax.axis_index("zh")) * NC + lax.axis_index("c")
    queries = q_ref[...].astype(f32)
    new_keys = nk_ref[...].astype(f32)
    new_values = nv_ref[...].astype(f32)
    for head in range(HEADS):
        g = head // group
        at = slice(head * tokens, (head + 1) * tokens)
        q_rows[at, :] = queries[:, head * HD : (head + 1) * HD]
        nk_rows[at, :] = new_keys[:, g * HD : (g + 1) * HD]
        nv_rows[at, :] = new_values[:, g * HD : (g + 1) * HD]
    all_lines = HEADS * tokens
    row = lax.broadcasted_iota(jnp.int32, (lines, tokens * span), 0) % tokens
    column = lax.broadcasted_iota(jnp.int32, (lines, tokens * span), 1)
    limit = jnp.zeros((lines, tokens * span), jnp.int32)
    for t in range(tokens):
        limit = jnp.where(row == t, length_ref[t], limit)
    live = (column // span == row) & (dev_index * span + column % span < limit)
    live = jnp.concatenate([live.astype(f32)] * KVH, axis=0) > 0.5
    lane = lax.broadcasted_iota(jnp.int32, (all_lines, HD), 1)
    first = dev_index == 0
    q = q_rows[...]
    scores = jnp.concatenate(
        [
            lax.dot_general(
                q[g * lines : (g + 1) * lines].astype(bf16),
                k_ref[:, g * HD : (g + 1) * HD],
                NT,
                preferred_element_type=f32,
            )
            for g in range(KVH)
        ],
        axis=0,
    )
    scores = jnp.where(live, scores * scale, DEAD)
    own = jnp.sum(q * nk_rows[...], axis=1, keepdims=True) * scale
    own = jnp.where(first, own, DEAD)
    top = jnp.maximum(jnp.max(scores, axis=1, keepdims=True), own)
    top_high = top.astype(bf16).astype(f32)
    top_low = (top - top_high).astype(bf16).astype(f32)
    base = top_high + top_low
    weights = jnp.where(live, jnp.exp(scores - base), 0.0).astype(bf16)
    own_weight = jnp.where(first, jnp.exp(own - base), 0.0).astype(bf16).astype(f32)
    acc = jnp.concatenate(
        [
            jnp.dot(
                weights[g * lines : (g + 1) * lines],
                v_ref[:, g * HD : (g + 1) * HD],
                preferred_element_type=f32,
            )
            for g in range(KVH)
        ],
        axis=0,
    )
    acc = acc + own_weight * nv_rows[...]
    total = jnp.sum(weights.astype(f32), axis=1, keepdims=True) + own_weight
    total_high = total.astype(bf16).astype(f32)
    total_low = total - total_high
    stats = jnp.where(
        lane == 0,
        top_high,
        jnp.where(
            lane == 1,
            top_low,
            jnp.where(lane == 2, total_high, jnp.where(lane == 3, total_low, 0.0)),
        ),
    )
    for x in range(NX):
        for z in range(NZ):
            for c in range(NC):
                to = slice(z * half, (z + 1) * half)
                at = ((x * NZ + z) * NC + c) * half
                packed[x * NC + c, to, :HD] = acc[at : at + half]
                packed[x * NC + c, to, HD:] = stats[at : at + half]
    one_hot = lax.broadcasted_iota(jnp.int32, (lines, HD), 0) == lane[:lines]
    one_hot = one_hot.astype(f32).astype(bf16)
    for x in range(NX):
        for c in range(NC):
            block = packed[x * NC + c].astype(bf16)
            turned = lax.dot_general(
                block[:, HD:], one_hot, (((0,), (0,)), ((), ())), preferred_element_type=f32
            )
            block = jnp.concatenate([packed[x * NC + c, :, :HD], turned[:8]], axis=0).astype(bf16)
            for z in range(NZ):
                out_ref[(x * NZ + z) * NC + c] = block


def enter_kernel(state_ref, gain_ref, own, other, out_ref):
    f32 = jnp.float32
    rows, span = state_ref.shape[1:]
    share = span // NZ
    hidden = own.shape[1]
    starts = starts_of(lax.axis_index("c"), share)
    squares = jnp.zeros((rows, HD), f32)
    sums = [jnp.zeros((rows, hidden), f32)] * (2 * NC)
    for x in range(NX):
        block = state_ref[x]
        for kind in range(2):
            for far, ref in enumerate((own, other)):
                sums[kind * NC + far] += lax.dot_general(
                    block, ref[kind, :, x * span : (x + 1) * span], NT, preferred_element_type=f32
                )
        gain = [gain_ref[:, pl.ds(s, share)] for s in starts[x * NZ : (x + 1) * NZ]]
        state = block.astype(f32) / jnp.concatenate(gain, axis=1)
        state = state * state
        for at in range(0, span, HD):
            squares += state[:, at : at + HD]
    total = jnp.sum(squares, axis=1, keepdims=True)
    total = jnp.broadcast_to(total, (rows, HD - hidden))
    for i in range(2 * NC):
        out_ref[i] = jnp.concatenate([sums[i], total], axis=1)


def leave_kernel(sums_ref, down_ref, other, out_ref):
    f32, bf16 = jnp.float32, jnp.bfloat16
    hidden, width = down_ref.shape
    share = out_ref.shape[3]
    at_c = lax.axis_index("c")
    factor = None
    active = []
    for far in range(NC):
        gate = sums_ref[at_c, far] + sums_ref[1 - at_c, 1 - far]
        up = sums_ref[at_c, NC + far] + sums_ref[1 - at_c, NC + 1 - far]
        if factor is None:
            factor = lax.rsqrt(gate[:, HD - 1 :] / width + 1e-05)
        gate = gate[:, :hidden] * factor
        up = up[:, :hidden] * factor
        active.append((gate / (1.0 + jnp.exp(-gate)) * up).astype(bf16))
    for i, start in enumerate(starts_of(at_c, share)):
        near = jnp.dot(active[0], down_ref[:, pl.ds(start, share)], preferred_element_type=f32)
        far = jnp.dot(active[1], other[2, :, i * share : (i + 1) * share], preferred_element_type=f32)
        out_ref[i // NZ, i % NZ] = (near + far).astype(bf16)


def local_attention(lengths, queries, key_cache, value_cache, new_key, new_value):
    rows, span, features = key_cache.shape
    slab_rows = HEADS // (NX * NC) * rows
    return pl.pallas_call(
        attend_kernel,
        out_shape=jax.ShapeDtypeStruct((NX * NZ * NC, slab_rows + 8, HD), jnp.bfloat16),
        in_specs=[pl.BlockSpec(memory_space=pltpu.SMEM)] + [pl.BlockSpec()] * 5,
        out_specs=VMEM,
        scratch_shapes=[pltpu.VMEM((HEADS * rows, HD), jnp.float32)] * 3
        + [pltpu.VMEM((NX * NC, slab_rows, 2 * HD), jnp.float32)],
        compiler_params=pltpu.CompilerParams(vmem_limit_bytes=60 * 2**20),
        name="attend",
    )(
        lengths,
        queries,
        key_cache.reshape(rows * span, features),
        value_cache.reshape(rows * span, features),
        new_key,
        new_value,
    )


def merge(arrived):
    f32 = jnp.float32
    lines = arrived.shape[1] - 8
    part = arrived[:, :lines].astype(f32)
    info = arrived[:, lines : lines + 4, :lines].astype(f32)
    base_of = info[:, 0] + info[:, 1]
    factor = jnp.exp(base_of - jnp.max(base_of, axis=0, keepdims=True))
    whole = jnp.sum(factor * (info[:, 2] + info[:, 3]), axis=0)
    return jnp.sum((factor / whole)[..., None] * part, axis=0)


def pack_weights(gate, up, down, experts, combine):
    rows = experts.shape[1]
    slots = jax.ShapeDtypeStruct((rows, EXPERTS * CAP), jnp.float32)
    hidden, width = down.shape
    return pl.pallas_call(
        pack_kernel,
        out_shape=tuple(
            jax.ShapeDtypeStruct((kinds, hidden, width // NC), jnp.bfloat16) for kinds in (2, 3)
        )
        + (slots, slots),
        in_specs=[ANY] * 5,
        out_specs=(ANY, ANY, VMEM, VMEM),
        scratch_shapes=[
            pltpu.VMEM((5, hidden, width // NC), jnp.bfloat16),
            pltpu.SMEM(experts.shape, jnp.int32),
            pltpu.SMEM(combine.shape, jnp.float32),
            pltpu.SemaphoreType.DMA((5, NX * NZ)),
            pltpu.SemaphoreType.DMA((5,)),
            pltpu.SemaphoreType.DMA((2,)),
        ],
        compiler_params=pltpu.CompilerParams(vmem_limit_bytes=52 * 2**20),
        name="pack",
    )(gate, up, down, experts, combine)


def expert_enter(state, gain, own, other):
    return pl.pallas_call(
        enter_kernel,
        out_shape=jax.ShapeDtypeStruct((2 * NC, state.shape[1], HD), jnp.float32),
        in_specs=[VMEM] * 4,
        out_specs=VMEM,
        compiler_params=pltpu.CompilerParams(vmem_limit_bytes=16 * 2**20),
        name="enter",
    )(state, gain, own, other)


def expert_leave(sums, down, other):
    share = down.shape[1] // (NX * NZ * NC)
    return pl.pallas_call(
        leave_kernel,
        out_shape=jax.ShapeDtypeStruct((NX, NZ, sums.shape[2], share), jnp.bfloat16),
        in_specs=[VMEM] * 3,
        out_specs=VMEM,
        compiler_params=pltpu.CompilerParams(vmem_limit_bytes=16 * 2**20),
        name="leave",
    )(sums, down, other)


def body(
    queries,
    key_cache,
    value_cache,
    new_key,
    new_value,
    lengths,
    experts,
    combine,
    residual,
    norm_gain,
    w_gate,
    w_up,
    w_down,
):
    bf16, f32 = jnp.bfloat16, jnp.float32
    rows, width = residual.shape
    dev_count = NX * NZ * NC
    outer_count = lax.axis_size("zl") * lax.axis_size("y")
    copies = outer_count // EXPERTS
    at_x, at_z, at_c = (lax.axis_index(a) for a in DEV)
    share = width // dev_count
    own_heads = HEADS // dev_count
    slots = outer_count * CAP

    packet = local_attention(lengths, queries, key_cache, value_cache, new_key, new_value)

    own, sent, place, mix = pack_weights(w_gate.T, w_up.T, w_down, experts.T, combine.T)
    other = lax.ppermute(sent, "c", [(0, 1), (1, 0)])
    arrived = lax.all_to_all(packet, DEV, split_axis=0, concat_axis=0, tiled=True)
    attended = merge(arrived)
    attended = jnp.transpose(attended.reshape(NZ, own_heads, rows, HD), (2, 0, 1, 3))
    attended = attended.reshape(rows, NZ, share)
    res = residual.reshape(rows, NX, NZ, NC, share)
    res = lax.dynamic_slice(res, (0, at_x, 0, at_c, 0), (rows, 1, NZ, 1, share))
    state = res.reshape(rows, NZ, share).astype(f32) + attended
    own_state = lax.dynamic_index_in_dim(state, at_z, 1, keepdims=False)
    gain = norm_gain.reshape(NX, NZ, NC, share)
    gain = lax.dynamic_slice(gain, (at_x, 0, at_c, 0), (1, NZ, 1, share)).reshape(1, NZ, share)
    scaled = (state * gain).reshape(rows, NZ * share).astype(bf16)

    packed = jnp.einsum(
        "rs,rd->sd", place.astype(bf16), scaled, preferred_element_type=f32
    ).astype(bf16)
    packed = packed.reshape(EXPERTS, CAP, NZ * share)
    outgoing = jnp.repeat(packed, copies, axis=0)
    outgoing, own_state = lax.optimization_barrier((outgoing, own_state))
    incoming = lax.all_to_all(outgoing, OUTER, split_axis=0, concat_axis=0, tiled=True)
    slab = incoming.reshape(slots, NZ * share)
    over_x = lax.all_gather(slab, "x", axis=0, tiled=False)
    sums = expert_enter(over_x, norm_gain.reshape(1, width), own, other)
    sums = lax.all_gather(sums, "c", axis=0, tiled=False)
    cut = expert_leave(sums, w_down, other)

    from_x = lax.all_to_all(cut, "x", split_axis=0, concat_axis=0, tiled=True)
    home = jnp.sum(from_x.astype(f32), axis=0).astype(bf16).reshape(NZ * outer_count, CAP, share)
    returned = lax.all_to_all(home, ("zh",) + OUTER, split_axis=0, concat_axis=0, tiled=True)
    returned = returned.reshape(NZ, EXPERTS, copies, CAP, share).astype(f32)
    expert_output = jnp.sum(returned, axis=(0, 2)).reshape(1, EXPERTS * CAP, share)
    moe = jnp.sum(mix.reshape(rows, EXPERTS * CAP, 1) * expert_output, axis=1)
    return (own_state + moe).astype(bf16)


def solution(mesh):
    fine = Mesh(mesh.devices.reshape(6, 8, NX, NZ, NC), OUTER + DEV)
    return jax.shard_map(
        body,
        mesh=fine,
        in_specs=(
            P(OUTER, None),
            P(OUTER, DEV, None),
            P(OUTER, DEV, None),
            P(OUTER, None),
            P(OUTER, None),
            P(OUTER),
            P(OUTER, None),
            P(OUTER, None),
            P(OUTER, None),
            P(),
            P(None, OUTER + DEV),
            P(None, OUTER + DEV),
            P(OUTER + DEV, None),
        ),
        out_specs=P(OUTER, DEV),
        check_vma=False,
    )
```

```python
import math

import jax
import jax.numpy as jnp
from jax import lax
from jax.experimental import pallas as pl
from jax.experimental.pallas import tpu as pltpu
from jax.sharding import Mesh
from jax.sharding import PartitionSpec as P

HEADS = 48
KVH = 8
HD = 128
EXPERTS = 8
TOPK = 2
CAP = 2
DEAD = -1e30

OUTER = ("zl", "y")
DEV = ("x", "zh", "c")
NX, NZ, NC = 4, 2, 2
ANY = pl.BlockSpec(memory_space=pl.ANY)
VMEM = pl.BlockSpec(memory_space=pltpu.VMEM)
NT = (((1,), (1,)), ((), ()))


def starts_of(core, share):
    return [pl.multiple_of((i * NC + core) * share, share) for i in range(NX * NZ)]


def pack_kernel(
    gate_ref,
    up_ref,
    down_ref,
    experts_ref,
    combine_ref,
    own_ref,
    out_ref,
    place_ref,
    mix_ref,
    stage,
    experts,
    combine,
    in_sems,
    out_sems,
    small_sems,
):
    share = gate_ref.shape[1] // (NX * NZ * NC)
    at_c = lax.axis_index("c")
    refs = (gate_ref, up_ref, down_ref)
    groups = []
    for to, core in ((out_ref, 1 - at_c), (own_ref, at_c)):
        for kind in range(to.shape[0]):
            slot = len(groups)
            copies = [
                pltpu.make_async_copy(
                    refs[kind].at[:, pl.ds(start, share)],
                    (stage if to is out_ref else own_ref).at[kind, :, pl.ds(i * share, share)],
                    in_sems.at[slot, i],
                )
                for i, start in enumerate(starts_of(core, share))
            ]
            leave = None
            if to is out_ref:
                leave = pltpu.make_async_copy(stage.at[kind], to.at[kind], out_sems.at[kind])
            groups.append((copies, leave))
    for copies, _ in groups:
        for copy in copies:
            copy.start()
    small = [
        pltpu.make_async_copy(experts_ref, experts, small_sems.at[0]),
        pltpu.make_async_copy(combine_ref, combine, small_sems.at[1]),
    ]
    for copy in small:
        copy.start()

    for copies, leave in groups:
        for copy in copies:
            copy.wait()
        if leave is not None:
            leave.start()

    for copy in small:
        copy.wait()
    choices = [(r, k) for r in range(place_ref.shape[0]) for k in range(TOPK)]
    chosen = [experts[k, r] for r, k in choices]
    row = lax.broadcasted_iota(jnp.int32, place_ref.shape, 0)
    column = lax.broadcasted_iota(jnp.int32, place_ref.shape, 1)
    place = jnp.zeros(place_ref.shape, jnp.float32)
    mix = jnp.zeros(place_ref.shape, jnp.float32)
    for i, (r, k) in enumerate(choices):
        rank = jnp.int32(0)
        for earlier in chosen[:i]:
            rank += jnp.where(earlier == chosen[i], 1, 0)
        hit = (row == r) & (column == chosen[i] * CAP + rank)
        place = jnp.where(hit, 1.0, place)
        mix = jnp.where(hit, combine[k, r], mix)
    place_ref[...] = place
    mix_ref[...] = mix

    for _, leave in groups:
        if leave is not None:
            leave.wait()


def attend_kernel(
    length_ref,
    q_ref,
    k_ref,
    v_ref,
    nk_ref,
    nv_ref,
    out_ref,
    q_rows,
    nk_rows,
    nv_rows,
    packed,
):
    f32, bf16 = jnp.float32, jnp.bfloat16
    tokens = q_ref.shape[0]
    span = k_ref.shape[0] // tokens
    group = HEADS // KVH
    lines = group * tokens
    half = lines // NC
    scale = 1.0 / math.sqrt(HD)
    dev_index = (lax.axis_index("x") * NZ + lax.axis_index("zh")) * NC + lax.axis_index("c")
    queries = q_ref[...].astype(f32)
    new_keys = nk_ref[...].astype(f32)
    new_values = nv_ref[...].astype(f32)
    for head in range(HEADS):
        g = head // group
        at = slice(head * tokens, (head + 1) * tokens)
        q_rows[at, :] = queries[:, head * HD : (head + 1) * HD]
        nk_rows[at, :] = new_keys[:, g * HD : (g + 1) * HD]
        nv_rows[at, :] = new_values[:, g * HD : (g + 1) * HD]
    all_lines = HEADS * tokens
    row = lax.broadcasted_iota(jnp.int32, (lines, tokens * span), 0) % tokens
    column = lax.broadcasted_iota(jnp.int32, (lines, tokens * span), 1)
    limit = jnp.zeros((lines, tokens * span), jnp.int32)
    for t in range(tokens):
        limit = jnp.where(row == t, length_ref[t], limit)
    live = (column // span == row) & (dev_index * span + column % span < limit)
    live = jnp.concatenate([live.astype(f32)] * KVH, axis=0) > 0.5
    lane = lax.broadcasted_iota(jnp.int32, (all_lines, HD), 1)
    first = dev_index == 0
    q = q_rows[...]
    scores = jnp.concatenate(
        [
            lax.dot_general(
                q[g * lines : (g + 1) * lines].astype(bf16),
                k_ref[:, g * HD : (g + 1) * HD],
                NT,
                preferred_element_type=f32,
            )
            for g in range(KVH)
        ],
        axis=0,
    )
    scores = jnp.where(live, scores * scale, DEAD)
    own = jnp.sum(q * nk_rows[...], axis=1, keepdims=True) * scale
    own = jnp.where(first, own, DEAD)
    top = jnp.maximum(jnp.max(scores, axis=1, keepdims=True), own)
    top_high = top.astype(bf16).astype(f32)
    top_low = (top - top_high).astype(bf16).astype(f32)
    base = top_high + top_low
    weights = jnp.where(live, jnp.exp(scores - base), 0.0).astype(bf16)
    own_weight = jnp.where(first, jnp.exp(own - base), 0.0).astype(bf16).astype(f32)
    acc = jnp.concatenate(
        [
            jnp.dot(
                weights[g * lines : (g + 1) * lines],
                v_ref[:, g * HD : (g + 1) * HD],
                preferred_element_type=f32,
            )
            for g in range(KVH)
        ],
        axis=0,
    )
    acc = acc + own_weight * nv_rows[...]
    total = jnp.sum(weights.astype(f32), axis=1, keepdims=True) + own_weight
    total_high = total.astype(bf16).astype(f32)
    total_low = total - total_high
    stats = jnp.where(
        lane == 0,
        top_high,
        jnp.where(
            lane == 1,
            top_low,
            jnp.where(lane == 2, total_high, jnp.where(lane == 3, total_low, 0.0)),
        ),
    )
    for x in range(NX):
        for z in range(NZ):
            for c in range(NC):
                to = slice(z * half, (z + 1) * half)
                at = ((x * NZ + z) * NC + c) * half
                packed[x * NC + c, to, :HD] = acc[at : at + half]
                packed[x * NC + c, to, HD:] = stats[at : at + half]
    one_hot = lax.broadcasted_iota(jnp.int32, (lines, HD), 0) == lane[:lines]
    one_hot = one_hot.astype(f32).astype(bf16)
    for x in range(NX):
        for c in range(NC):
            block = packed[x * NC + c].astype(bf16)
            turned = lax.dot_general(
                block[:, HD:], one_hot, (((0,), (0,)), ((), ())), preferred_element_type=f32
            )
            block = jnp.concatenate([packed[x * NC + c, :, :HD], turned[:8]], axis=0).astype(bf16)
            for z in range(NZ):
                out_ref[(x * NZ + z) * NC + c] = block


def enter_kernel(state_ref, gain_ref, own, other, out_ref):
    f32 = jnp.float32
    rows, span = state_ref.shape[1:]
    share = span // NZ
    hidden = own.shape[1]
    starts = starts_of(lax.axis_index("c"), share)
    squares = jnp.zeros((rows, HD), f32)
    sums = [jnp.zeros((rows, hidden), f32)] * (2 * NC)
    for x in range(NX):
        block = state_ref[x]
        for kind in range(2):
            for far, ref in enumerate((own, other)):
                sums[kind * NC + far] += lax.dot_general(
                    block, ref[kind, :, x * span : (x + 1) * span], NT, preferred_element_type=f32
                )
        gain = [gain_ref[:, pl.ds(s, share)] for s in starts[x * NZ : (x + 1) * NZ]]
        state = block.astype(f32) / jnp.concatenate(gain, axis=1)
        state = state * state
        for at in range(0, span, HD):
            squares += state[:, at : at + HD]
    total = jnp.sum(squares, axis=1, keepdims=True)
    total = jnp.broadcast_to(total, (rows, HD - hidden))
    for i in range(2 * NC):
        out_ref[i] = jnp.concatenate([sums[i], total], axis=1)


def leave_kernel(sums_ref, down_ref, other, out_ref):
    f32, bf16 = jnp.float32, jnp.bfloat16
    hidden, width = down_ref.shape
    share = out_ref.shape[3]
    at_c = lax.axis_index("c")
    factor = None
    active = []
    for far in range(NC):
        gate = sums_ref[at_c, far] + sums_ref[1 - at_c, 1 - far]
        up = sums_ref[at_c, NC + far] + sums_ref[1 - at_c, NC + 1 - far]
        if factor is None:
            factor = lax.rsqrt(gate[:, HD - 1 :] / width + 1e-05)
        gate = gate[:, :hidden] * factor
        up = up[:, :hidden] * factor
        active.append((gate / (1.0 + jnp.exp(-gate)) * up).astype(bf16))
    for i, start in enumerate(starts_of(at_c, share)):
        near = jnp.dot(active[0], down_ref[:, pl.ds(start, share)], preferred_element_type=f32)
        far = jnp.dot(active[1], other[2, :, i * share : (i + 1) * share], preferred_element_type=f32)
        out_ref[i // NZ, i % NZ] = (near + far).astype(bf16)


def local_attention(lengths, queries, key_cache, value_cache, new_key, new_value):
    rows, span, features = key_cache.shape
    slab_rows = HEADS // (NX * NC) * rows
    return pl.pallas_call(
        attend_kernel,
        out_shape=jax.ShapeDtypeStruct((NX * NZ * NC, slab_rows + 8, HD), jnp.bfloat16),
        in_specs=[pl.BlockSpec(memory_space=pltpu.SMEM)] + [pl.BlockSpec()] * 5,
        out_specs=VMEM,
        scratch_shapes=[pltpu.VMEM((HEADS * rows, HD), jnp.float32)] * 3
        + [pltpu.VMEM((NX * NC, slab_rows, 2 * HD), jnp.float32)],
        compiler_params=pltpu.CompilerParams(vmem_limit_bytes=60 * 2**20),
        name="attend",
    )(
        lengths,
        queries,
        key_cache.reshape(rows * span, features),
        value_cache.reshape(rows * span, features),
        new_key,
        new_value,
    )


def merge(arrived):
    f32 = jnp.float32
    lines = arrived.shape[1] - 8
    part = arrived[:, :lines].astype(f32)
    info = arrived[:, lines : lines + 4, :lines].astype(f32)
    base_of = info[:, 0] + info[:, 1]
    factor = jnp.exp(base_of - jnp.max(base_of, axis=0, keepdims=True))
    whole = jnp.sum(factor * (info[:, 2] + info[:, 3]), axis=0)
    return jnp.sum((factor / whole)[..., None] * part, axis=0)


def pack_weights(gate, up, down, experts, combine):
    rows = experts.shape[1]
    slots = jax.ShapeDtypeStruct((rows, EXPERTS * CAP), jnp.float32)
    hidden, width = down.shape
    return pl.pallas_call(
        pack_kernel,
        out_shape=tuple(
            jax.ShapeDtypeStruct((kinds, hidden, width // NC), jnp.bfloat16) for kinds in (2, 3)
        )
        + (slots, slots),
        in_specs=[ANY] * 5,
        out_specs=(ANY, ANY, VMEM, VMEM),
        scratch_shapes=[
            pltpu.VMEM((3, hidden, width // NC), jnp.bfloat16),
            pltpu.SMEM(experts.shape, jnp.int32),
            pltpu.SMEM(combine.shape, jnp.float32),
            pltpu.SemaphoreType.DMA((5, NX * NZ)),
            pltpu.SemaphoreType.DMA((3,)),
            pltpu.SemaphoreType.DMA((2,)),
        ],
        compiler_params=pltpu.CompilerParams(vmem_limit_bytes=52 * 2**20),
        name="pack",
    )(gate, up, down, experts, combine)


def expert_enter(state, gain, own, other):
    return pl.pallas_call(
        enter_kernel,
        out_shape=jax.ShapeDtypeStruct((2 * NC, state.shape[1], HD), jnp.float32),
        in_specs=[VMEM] * 4,
        out_specs=VMEM,
        compiler_params=pltpu.CompilerParams(vmem_limit_bytes=16 * 2**20),
        name="enter",
    )(state, gain, own, other)


def expert_leave(sums, down, other):
    share = down.shape[1] // (NX * NZ * NC)
    return pl.pallas_call(
        leave_kernel,
        out_shape=jax.ShapeDtypeStruct((NX, NZ, sums.shape[2], share), jnp.bfloat16),
        in_specs=[VMEM] * 3,
        out_specs=VMEM,
        compiler_params=pltpu.CompilerParams(vmem_limit_bytes=16 * 2**20),
        name="leave",
    )(sums, down, other)


def body(
    queries,
    key_cache,
    value_cache,
    new_key,
    new_value,
    lengths,
    experts,
    combine,
    residual,
    norm_gain,
    w_gate,
    w_up,
    w_down,
):
    bf16, f32 = jnp.bfloat16, jnp.float32
    rows, width = residual.shape
    dev_count = NX * NZ * NC
    outer_count = lax.axis_size("zl") * lax.axis_size("y")
    copies = outer_count // EXPERTS
    at_x, at_z, at_c = (lax.axis_index(a) for a in DEV)
    share = width // dev_count
    own_heads = HEADS // dev_count
    slots = outer_count * CAP

    packet = local_attention(lengths, queries, key_cache, value_cache, new_key, new_value)

    own, sent, place, mix = pack_weights(w_gate.T, w_up.T, w_down, experts.T, combine.T)
    other = lax.ppermute(sent, "c", [(0, 1), (1, 0)])
    arrived = lax.all_to_all(packet, DEV, split_axis=0, concat_axis=0, tiled=True)
    attended = merge(arrived)
    attended = jnp.transpose(attended.reshape(NZ, own_heads, rows, HD), (2, 0, 1, 3))
    attended = attended.reshape(rows, NZ, share)
    res = residual.reshape(rows, NX, NZ, NC, share)
    res = lax.dynamic_slice(res, (0, at_x, 0, at_c, 0), (rows, 1, NZ, 1, share))
    state = res.reshape(rows, NZ, share).astype(f32) + attended
    own_state = lax.dynamic_index_in_dim(state, at_z, 1, keepdims=False)
    gain = norm_gain.reshape(NX, NZ, NC, share)
    gain = lax.dynamic_slice(gain, (at_x, 0, at_c, 0), (1, NZ, 1, share)).reshape(1, NZ, share)
    scaled = (state * gain).reshape(rows, NZ * share).astype(bf16)

    packed = jnp.einsum(
        "rs,rd->sd", place.astype(bf16), scaled, preferred_element_type=f32
    ).astype(bf16)
    packed = packed.reshape(EXPERTS, CAP, NZ * share)
    outgoing = jnp.repeat(packed, copies, axis=0)
    outgoing, own_state = lax.optimization_barrier((outgoing, own_state))
    incoming = lax.all_to_all(outgoing, OUTER, split_axis=0, concat_axis=0, tiled=True)
    slab = incoming.reshape(slots, NZ * share)
    over_x = lax.all_gather(slab, "x", axis=0, tiled=False)
    sums = expert_enter(over_x, norm_gain.reshape(1, width), own, other)
    sums = lax.all_gather(sums, "c", axis=0, tiled=False)
    cut = expert_leave(sums, w_down, other)

    from_x = lax.all_to_all(cut, "x", split_axis=0, concat_axis=0, tiled=True)
    home = jnp.sum(from_x.astype(f32), axis=0).astype(bf16).reshape(NZ * outer_count, CAP, share)
    returned = lax.all_to_all(home, ("zh",) + OUTER, split_axis=0, concat_axis=0, tiled=True)
    returned = returned.reshape(NZ, EXPERTS, copies, CAP, share).astype(f32)
    expert_output = jnp.sum(returned, axis=(0, 2)).reshape(1, EXPERTS * CAP, share)
    moe = jnp.sum(mix.reshape(rows, EXPERTS * CAP, 1) * expert_output, axis=1)
    return (own_state + moe).astype(bf16)


def solution(mesh):
    fine = Mesh(mesh.devices.reshape(6, 8, NX, NZ, NC), OUTER + DEV)
    return jax.shard_map(
        body,
        mesh=fine,
        in_specs=(
            P(OUTER, None),
            P(OUTER, DEV, None),
            P(OUTER, DEV, None),
            P(OUTER, None),
            P(OUTER, None),
            P(OUTER),
            P(OUTER, None),
            P(OUTER, None),
            P(OUTER, None),
            P(),
            P(None, OUTER + DEV),
            P(None, OUTER + DEV),
            P(OUTER + DEV, None),
        ),
        out_specs=P(OUTER, DEV),
        check_vma=False,
    )
```
